256 devices in a mesh: dp: 4 (over y), expert: 64 (over z, x, core).
Axes of the slice: x: 4, y: 4, z: 8, core: 2. Of those that a mesh axis runs over, the one named last changes fastest.
Arguments:
- tokens: bfloat16 [8192, 4096], P('expert', 'dp'), may hold values from -6 to 6
- grad_out: bfloat16 [8192, 4096], P('expert', 'dp'), may hold values from -6 to 6
- route_weights: bfloat16 [8192, 2], P('expert'), may hold values from 0.049804688 to 1
- expert_ids: int32 [8192, 2], P('expert'), may hold values from 0 to 63, all different within a row; in each aligned block of 128 rows (0 to 127, 128 to 255, ...) at most 8 rows name the same one
- gate_weight: bfloat16 [64, 4096, 1024], P('expert', None, 'dp'), may hold values from -0.09375 to 0.09375
- up_weight: bfloat16 [64, 4096, 1024], P('expert', None, 'dp'), may hold values from -0.09375 to 0.09375
- down_weight: bfloat16 [64, 1024, 4096], P('expert', 'dp'), may hold values from -0.1875 to 0.1875
Outputs:
- grad_tokens: bfloat16 [8192, 4096], P('expert', 'dp')
- grad_gate: bfloat16 [64, 4096, 1024], P('expert', None, 'dp')
- grad_up: bfloat16 [64, 4096, 1024], P('expert', None, 'dp')
- grad_down: bfloat16 [64, 1024, 4096], P('expert', 'dp')
The draws below stay inside these ranges and needn't reach their ends.
Inputs may be any that keep to these rules, and one draw needn't show every extreme that they name: `expert_ids`: each row names 2 different experts. Among the 128 rows of one device no expert is named more than 8 times, and in some such block an expert is named exactly 8 times.
All inputs are finite; a program needn't handle non-finite values.
Results may differ from the reference program's by a relative error of at most 0.0057.
Values may be sent and summed in bfloat16 or wider, within the bound.
A program may use at most 128 MiB of HBM per device.

```python
import math
import jax
import jax.numpy as jnp
import numpy as np
from jax import lax

D = 4096
FF = 1024
TOP = 2
TOK_DEV = 128
EXPERTS = 64
TOKENS = 8192
CAP = 8


def shard_levels(rng, shape, split, least, top_value):
    factor_of, own = 1.0, jax.random.fold_in(rng, 6)
    for axis_at, shards_of in split:
        heights = jnp.exp(jax.random.uniform(jax.random.fold_in(own, axis_at), (shards_of,), jnp.float32, least / len(split), top_value / len(split)))
        factor_of = factor_of * jnp.repeat(heights, shape[axis_at] // shards_of).reshape([-1 if axis == axis_at else 1 for axis in range(len(shape))])
    return factor_of


def shared_out(own_key, own, number, rows, number_of, top, bound, lean):
    order = jax.random.permutation(own_key, number_of)
    heavy_load, ordinary = portions_of(number_of, rows * top, bound, lean, True), portions_of(number_of, rows * top, bound, lean, False)
    places = jnp.arange(number_of)

    def named(lengths, offset_by):
        used = int((lengths > 0).sum())
        fixed = max(1, used // 4)
        moved = fixed + (places - fixed + offset_by * (used - fixed)) % max(1, number_of - fixed)
        return jnp.zeros((number_of,), jnp.int32).at[order[jnp.where(places < fixed, places, moved)]].set(jnp.asarray(lengths, jnp.int32))

    lengths = jnp.where(number % 4 == 0, named(heavy_load, number // 4), named(ordinary, number - number // 4 - 1))
    mixed = jax.random.permutation(jax.random.fold_in(own, 3), number_of)
    donor, receiver = mixed[0:number_of // 2 * 2:2], mixed[1:number_of // 2 * 2:2]
    slack = jnp.minimum(lengths[donor] - 1, bound - lengths[receiver]) // 2
    slack = jnp.where((donor == order[0]) | (receiver == order[0]) | (lengths[receiver] == 0), 0, jnp.maximum(slack, 0))
    moved = jax.random.randint(jax.random.fold_in(own, 4), (number_of // 2,), 0, 1 << 20) % (slack + 1)
    lengths = lengths.at[donor].add(-moved).at[receiver].add(moved)
    members = jnp.searchsorted(jnp.cumsum(lengths), jnp.arange(rows * top), side="right").astype(jnp.int32)
    table = members.reshape(top, rows).T
    table = table[jax.random.permutation(jax.random.fold_in(own, 1), rows)]
    offset_by = jax.random.randint(jax.random.fold_in(own, 2), (rows, 1), 0, top)
    return jnp.take_along_axis(table, (jnp.arange(top)[None, :] + offset_by) % top, axis=1)


def portions_of(amount, total, bound, skew, full):
    portions = [(1 << 20) // math.isqrt(standing ** skew) + 1 for standing in range(1, amount + 1)]
    largest = bound if full else min(bound, max(-(-total // amount), total * portions[0] // sum(portions)))
    least = 1 if total - largest >= amount - 1 else 0
    given, rest = [largest] + [least] * (amount - 1), total - largest - least * (amount - 1)
    while rest > 0:
        candidates = [i for i in range(1, amount) if given[i] < largest] or [i for i in range(1, amount) if given[i] < bound]
        whole, remaining = sum([portions[i] for i in candidates]), rest
        for i in candidates:
            extra = min(bound - given[i], max(1, remaining * portions[i] // whole), rest)
            given[i] = given[i] + extra
            rest = rest - extra
    return np.array(given)


def centred(key, dims, spread, most, split=(), kind=jnp.bfloat16):
    array = spread * jax.random.normal(key, dims, jnp.float32)
    if split:
        array = array * shard_levels(key, dims, split, -0.22, 0.18)
    return jnp.clip(array, -most, most).astype(kind)


def setup_inputs(seed: int = 0) -> dict:
    keys = jax.random.split(jax.random.key(seed), 8)
    tokens = centred(keys[0], (TOKENS, D), 1.0, 6.0, ((0, 64), (1, 4)))
    grad_out = centred(keys[1], (TOKENS, D), 1.0, 6.0, ((0, 64), (1, 4)))
    route_weights = jnp.clip(0.049804688 + 0.9501953 * jax.random.uniform(keys[2], (TOKENS, TOP), jnp.float32) ** shard_levels(keys[2], (TOKENS, TOP), ((0, 64),), -0.2, 0.2), 0.049804688, 1.0).astype(jnp.bfloat16)
    expert_ids_keys = jax.random.split(jax.random.fold_in(keys[3], 1), TOKENS // TOK_DEV)
    expert_ids_turns = jax.random.permutation(jax.random.fold_in(keys[3], 3), TOKENS // TOK_DEV)
    expert_ids = jax.vmap(lambda own, number: shared_out(jax.random.fold_in(keys[3], 2), own, number, TOK_DEV, EXPERTS, TOP, CAP, 2))(expert_ids_keys, expert_ids_turns).reshape((TOKENS, TOP))
    gate_weight = centred(keys[4], (EXPERTS, D, FF), D ** -0.5, 0.09375, ((0, 64), (2, 4)))
    up_weight = centred(keys[5], (EXPERTS, D, FF), D ** -0.5, 0.09375, ((0, 64), (2, 4)))
    down_weight = centred(keys[6], (EXPERTS, FF, D), FF ** -0.5, 0.1875, ((0, 64), (1, 4)))
    return {"tokens": tokens, "grad_out": grad_out, "route_weights": route_weights, "expert_ids": expert_ids, "gate_weight": gate_weight, "up_weight": up_weight, "down_weight": down_weight}


def expert_backward(rows_in, rows_grad, rows_weight, gate_matrix, up_matrix, down_matrix):
    gate_pre = jnp.dot(rows_in, gate_matrix, preferred_element_type=jnp.float32)
    up_pre = jnp.dot(rows_in, up_matrix, preferred_element_type=jnp.float32)
    sigmoid_gate = jax.nn.sigmoid(gate_pre)
    swish_gate = gate_pre * sigmoid_gate
    activated = (swish_gate * up_pre).astype(jnp.bfloat16)
    scaled = (rows_weight[:, None].astype(jnp.float32) * rows_grad.astype(jnp.float32)).astype(jnp.bfloat16)
    grad_act = jnp.dot(scaled, down_matrix.T, preferred_element_type=jnp.float32)
    grad_gate_pre = (grad_act * up_pre * sigmoid_gate * (1.0 + gate_pre * (1.0 - sigmoid_gate))).astype(jnp.bfloat16)
    grad_up_pre = (grad_act * swish_gate).astype(jnp.bfloat16)
    grad_down = jnp.dot(activated.T, scaled, preferred_element_type=jnp.float32).astype(jnp.bfloat16)
    grad_gate = jnp.dot(rows_in.T, grad_gate_pre, preferred_element_type=jnp.float32).astype(jnp.bfloat16)
    grad_up = jnp.dot(rows_in.T, grad_up_pre, preferred_element_type=jnp.float32).astype(jnp.bfloat16)
    back_terms = jnp.dot(grad_gate_pre, gate_matrix.T, preferred_element_type=jnp.float32)
    back_terms = back_terms + jnp.dot(grad_up_pre, up_matrix.T, preferred_element_type=jnp.float32)
    return grad_gate, grad_up, grad_down, back_terms


def reference(tokens, grad_out, route_weights, expert_ids, gate_weight, up_weight, down_weight):
    blocks = TOKENS // TOK_DEV
    per_block = TOK_DEV * TOP
    routed = expert_ids.reshape(blocks, per_block)
    onehot = (routed[:, :, None] == jnp.arange(EXPERTS, dtype=jnp.int32)[None, None, :]).astype(jnp.int32)
    earlier = jnp.cumsum(onehot, axis=1) - onehot
    slot_index = jnp.sum(earlier * onehot, axis=2).astype(jnp.int32)
    offsets = (jnp.arange(blocks, dtype=jnp.int32) * (EXPERTS * CAP))[:, None]
    target = (offsets + routed * CAP + slot_index).reshape(-1).astype(jnp.int32)
    assignments = blocks * per_block
    slot_table = jnp.full((blocks * EXPERTS * CAP,), -1, dtype=jnp.int32)
    slot_table = slot_table.at[target].set(jnp.arange(assignments, dtype=jnp.int32))
    slot_table = slot_table.reshape(blocks, EXPERTS, CAP)
    flat_weights = route_weights.reshape(-1)

    def accumulate(summed_rows, inputs):
        expert_index, gate_matrix, up_matrix, down_matrix = inputs
        chosen = lax.dynamic_index_in_dim(slot_table, expert_index, axis=1, keepdims=False).reshape(-1)
        is_valid = chosen >= 0
        assign_index = jnp.where(is_valid, chosen, 0).astype(jnp.int32)
        owner_row = (assign_index // TOP).astype(jnp.int32)
        rows_in = jnp.where(is_valid[:, None], tokens[owner_row], jnp.zeros((), tokens.dtype))
        rows_grad = jnp.where(is_valid[:, None], grad_out[owner_row], jnp.zeros((), grad_out.dtype))
        rows_weight = jnp.where(is_valid, flat_weights[assign_index], jnp.zeros((), route_weights.dtype))
        grad_gate, grad_up, grad_down, back_terms = expert_backward(rows_in, rows_grad, rows_weight, gate_matrix, up_matrix, down_matrix)
        summed_rows = summed_rows.at[owner_row].add(back_terms)
        return summed_rows, (grad_gate, grad_up, grad_down)

    initial = jnp.zeros((TOKENS, D), jnp.float32)
    summed_rows, outputs = lax.scan(accumulate, initial, (jnp.arange(EXPERTS, dtype=jnp.int32), gate_weight, up_weight, down_weight))
    grad_gate, grad_up, grad_down = outputs
    return summed_rows.astype(jnp.bfloat16), grad_gate, grad_up, grad_down
```

```python
import functools

import jax
import jax.numpy as jnp
from jax import lax
from jax.experimental import pallas as pl
from jax.experimental.pallas import tpu as pltpu
from jax.sharding import PartitionSpec as P

CAP = 8
PARTS = 4
ZS, XS, CORES = 8, 4, 2
MESH = pl.DeviceIdType.MESH


def dot_last(left, right):
    return lax.dot_general(
        left, right, (((1,), (1,)), ((), ())), preferred_element_type=jnp.float32
    )


def dot_rows(left, right):
    return lax.dot_general(
        left, right, (((0,), (0,)), ((), ())), preferred_element_type=jnp.float32
    )


def kernel(
    ids_ref, weights_ref, tokens_ref, grad_ref, gate_hbm, up_hbm, down_hbm,
    out_tokens, out_gate, out_up, out_down,
    both, send, recv, tok, sca, wgu, wdn, hid, act, part,
    pair_send, pair_recv, sum_send, sum_recv, home_send, home,
    stage_gate, stage_up, stage_down,
    weight_sems, send_sems, recv_sems, own_send, fwd_send, row_sems,
    pair_out, pair_sems, sum_out, sum_sems, home_out, home_sem, write_sems,
):
    rank = lax.axis_index("expert")
    y = lax.axis_index("dp")
    plane = XS * CORES
    experts = ZS * plane
    rows = plane * CAP
    zi, xi, ci = rank // plane, (rank // CORES) % XS, rank % CORES
    right, left = (y + 1) % PARTS, (y + PARTS - 1) % PARTS
    across = (y + 2) % PARTS
    tok_rows, width = tokens_ref.shape
    half = width // 2
    hidden = act.shape[1]

    def at(row, col):
        return pl.ds(pl.multiple_of(row * col, col), col)

    def offset(k):
        return (k * (2 * (k % 2) - 1) + ZS * ZS) % ZS

    def peer(k, i, sign):
        z = (zi + sign * offset(k) + ZS) % ZS
        x = (xi + sign * (i // CORES) + XS) % XS
        c = (ci + i) % CORES
        return z * plane + x * CORES + c

    barrier = pltpu.get_barrier_semaphore()

    def greet(j, carry):
        pl.semaphore_signal(
            barrier, inc=1, device_id=(y, (rank + j) % experts), device_id_type=MESH
        )
        return carry

    lax.fori_loop(1, experts, greet, 0)
    for side in (left, right):
        pl.semaphore_signal(barrier, inc=1, device_id=(side, rank), device_id_type=MESH)

    weight_copies = [
        pltpu.make_async_copy(gate_hbm, wgu.at[:, pl.ds(0, hidden)], weight_sems.at[0]),
        pltpu.make_async_copy(up_hbm, wgu.at[:, pl.ds(hidden, hidden)], weight_sems.at[1]),
        pltpu.make_async_copy(down_hbm, wdn, weight_sems.at[2]),
    ]
    for copy in weight_copies:
        copy.start()

    both[pl.ds(0, tok_rows), :] = tokens_ref[...]
    both[pl.ds(tok_rows, tok_rows), :] = grad_ref[...]

    ids, weights = ids_ref[...], weights_ref[...].astype(jnp.float32)
    numbers = lax.broadcasted_iota(jnp.int32, (experts, tok_rows), 0)
    hits = [numbers == ids[c : c + 1] for c in range(2)]
    before = lax.broadcasted_iota(jnp.int32, (tok_rows, tok_rows), 0) < (
        lax.broadcasted_iota(jnp.int32, (tok_rows, tok_rows), 1)
    )
    earlier = jnp.dot(
        jnp.where(hits[0] | hits[1], 1.0, 0.0).astype(jnp.bfloat16),
        jnp.where(before, 1.0, 0.0).astype(jnp.bfloat16),
        preferred_element_type=jnp.float32,
    )
    place = [
        jnp.sum(jnp.where(hits[c], earlier, 0.0), axis=0, keepdims=True)
        + ids[c : c + 1].astype(jnp.float32) * (2 * CAP)
        for c in range(2)
    ]

    def chosen(z, first, second):
        line = lax.broadcasted_iota(jnp.int32, (plane * 2 * CAP, tok_rows), 0)
        line = (line + z * (plane * 2 * CAP)).astype(jnp.float32)
        halves = [
            jnp.where(line == place[0] + shift, value[0:1], 0.0)
            + jnp.where(line == place[1] + shift, value[1:2], 0.0)
            for shift, value in ((0.0, first), (float(CAP), second))
        ]
        return jnp.concatenate(halves, axis=1).astype(jnp.bfloat16)

    ones = jnp.ones_like(weights)

    def pack(k):
        z = (zi - offset(k) + ZS) % ZS
        picked = jnp.dot(
            chosen(z, ones, weights), both[...], preferred_element_type=jnp.float32
        )
        send[at(z, plane)] = picked.astype(jnp.bfloat16).reshape(plane, 2 * CAP, width)

    def row_copy(k, i):
        target = peer(k, i, -1)
        return pltpu.make_async_remote_copy(
            src_ref=send.at[target],
            dst_ref=recv.at[k * plane + i],
            send_sem=send_sems.at[k],
            recv_sem=recv_sems.at[k],
            device_id=(y, target),
            device_id_type=MESH,
        )

    def dispatch(k, first):
        def one(i, carry):
            row_copy(k, i).start()
            return carry

        lax.fori_loop(first, plane, one, 0)

    def block_wait(k, count):
        return pltpu.make_async_remote_copy(
            src_ref=send.at[pl.ds(0, count)],
            dst_ref=recv.at[pl.ds(k * plane + plane - count, count)],
            send_sem=send_sems.at[k],
            recv_sem=recv_sems.at[k],
            device_id=(right, rank),
            device_id_type=MESH,
        )

    def side_copy(buf, q, k, sem_out, sem_in, side):
        block = buf.at[q, at(k, rows)]
        return pltpu.make_async_remote_copy(
            src_ref=block,
            dst_ref=block,
            send_sem=sem_out,
            recv_sem=sem_in,
            device_id=(side, rank),
            device_id_type=MESH,
        )

    def own_copies(k):
        return [
            side_copy(tok, y, k, own_send.at[0, k], row_sems.at[0, k], right),
            side_copy(sca, y, k, own_send.at[3, k], row_sems.at[3, k], left),
            side_copy(sca, y, k, own_send.at[1, k], row_sems.at[1, k], right),
            side_copy(tok, y, k, own_send.at[2, k], row_sems.at[2, k], left),
        ]

    def onward_copies(k):
        return [
            side_copy(tok, left, k, fwd_send.at[0, k], row_sems.at[4, k], right),
            side_copy(sca, right, k, fwd_send.at[1, k], row_sems.at[5, k], left),
        ]

    def spread(k):
        @pl.when(k == 0)
        def _():
            block_wait(0, plane - 1).wait_recv()

        @pl.when(k > 0)
        def _():
            block_wait(k, plane).wait_recv()

        got = recv[at(k, plane)].astype(jnp.float32)
        mine = at(k, rows)
        tok[y, mine, :] = got[:, :CAP, :].reshape(rows, width).astype(jnp.bfloat16)
        sca[y, mine, :] = got[:, CAP:, :].reshape(rows, width).astype(jnp.bfloat16)
        for copy in own_copies(k):
            copy.start()

    def onward(k):
        copies = onward_copies(k)
        side_copy(tok, left, k, own_send.at[0, k], row_sems.at[0, k], right).wait_recv()
        copies[0].start()
        side_copy(sca, right, k, own_send.at[3, k], row_sems.at[3, k], left).wait_recv()
        copies[1].start()

    def pair_copy(s, k, side):
        return pltpu.make_async_remote_copy(
            src_ref=pair_send.at[s, k],
            dst_ref=pair_recv.at[s, k],
            send_sem=pair_out.at[s, k],
            recv_sem=pair_sems.at[s, k],
            device_id=(side, rank),
            device_id_type=MESH,
        )

    def sum_copy(s, k, side):
        return pltpu.make_async_remote_copy(
            src_ref=sum_send.at[s, k],
            dst_ref=sum_recv.at[s, k],
            send_sem=sum_out.at[s, k],
            recv_sem=sum_sems.at[s, k],
            device_id=(side, rank),
            device_id_type=MESH,
        )

    def back_part(k, q):
        mine = at(k, rows)
        return dot_last(hid[mine, :], wgu[at(q, width), :])

    def compute(k):
        mine = at(k, rows)
        side_copy(sca, left, k, own_send.at[1, k], row_sems.at[1, k], right).wait_recv()
        side_copy(tok, right, k, own_send.at[2, k], row_sems.at[2, k], left).wait_recv()
        side_copy(tok, across, k, fwd_send.at[0, k], row_sems.at[4, k], right).wait_recv()
        side_copy(sca, across, k, fwd_send.at[1, k], row_sems.at[5, k], left).wait_recv()
        pre = jnp.zeros((rows, 2 * hidden), jnp.float32)
        grad_act = jnp.zeros((rows, hidden), jnp.float32)
        for q in range(PARTS):
            pre += jnp.dot(
                tok[q, mine, :], wgu[pl.ds(q * width, width), :],
                preferred_element_type=jnp.float32,
            )
            grad_act += dot_last(sca[q, mine, :], wdn[:, pl.ds(q * width, width)])
        gate_pre, up_pre = pre[:, :hidden], pre[:, hidden:]
        sigmoid_gate = 1.0 / (1.0 + jnp.exp(-gate_pre))
        swish_gate = gate_pre * sigmoid_gate
        act[mine, :] = (swish_gate * up_pre).astype(jnp.bfloat16)
        hid[mine, :] = jnp.concatenate(
            [
                grad_act * up_pre * sigmoid_gate * (1.0 + gate_pre * (1.0 - sigmoid_gate)),
                grad_act * swish_gate,
            ],
            axis=1,
        ).astype(jnp.bfloat16)
        far = back_part(k, across).astype(jnp.bfloat16)
        pair_send[0, k] = far[:, :half]
        pair_send[1, k] = far[:, half:]
        pair_copy(0, k, right).start()
        pair_copy(1, k, left).start()
        part[0, mine, :] = back_part(k, right)
        part[1, mine, :] = back_part(k, left)
        part[2, mine, :] = back_part(k, y)

    def reduce_sides(k):
        mine = at(k, rows)
        pair_copy(0, k, right).wait_recv()
        near = part[0, mine, :]
        sum_send[0, k] = jnp.concatenate(
            [near[:, :half] + pair_recv[0, k].astype(jnp.float32), near[:, half:]], axis=1
        ).astype(jnp.bfloat16)
        sum_copy(0, k, right).start()
        pair_copy(1, k, left).wait_recv()
        near = part[1, mine, :]
        sum_send[1, k] = jnp.concatenate(
            [near[:, :half], near[:, half:] + pair_recv[1, k].astype(jnp.float32)], axis=1
        ).astype(jnp.bfloat16)
        sum_copy(1, k, left).start()

    def home_copy(k, i):
        target = peer(k, i, 1)
        return pltpu.make_async_remote_copy(
            src_ref=home_send.at[k * plane + i],
            dst_ref=home.at[rank],
            send_sem=home_out.at[k],
            recv_sem=home_sem.at[0],
            device_id=(y, target),
            device_id_type=MESH,
        )

    def go_home(k):
        mine = at(k, rows)
        sum_copy(0, k, right).wait_recv()
        sum_copy(1, k, left).wait_recv()
        total = (
            part[2, mine, :]
            + sum_recv[0, k].astype(jnp.float32)
            + sum_recv[1, k].astype(jnp.float32)
        ).reshape(plane, CAP, width)
        home_send[at(k, plane)] = jnp.concatenate(
            [total[:, :, :half], total[:, :, half:]], axis=1
        ).astype(jnp.bfloat16)

        def one(i, carry):
            home_copy(k, i).start()
            return carry

        @pl.when(k == 0)
        def _():
            home[rank] = home_send[0]
            lax.fori_loop(1, plane, one, 0)

        @pl.when(k > 0)
        def _():
            lax.fori_loop(0, plane, one, 0)

    def write_copies(q):
        lines = pl.ds(pl.multiple_of(q * width, width), width)
        return [
            pltpu.make_async_copy(stage_gate.at[lines], out_gate.at[lines], write_sems.at[0, q]),
            pltpu.make_async_copy(stage_up.at[lines], out_up.at[lines], write_sems.at[1, q]),
            pltpu.make_async_copy(
                stage_down.at[:, lines], out_down.at[:, lines], write_sems.at[2, q]
            ),
        ]

    def weight_grads(q):
        tile = min(256, width)

        def one(j, carry):
            cols = at(j, tile)
            lines = pl.ds(pl.multiple_of(q * width + j * tile, tile), tile)
            grads = dot_rows(tok[q, :, cols], hid[...]).astype(jnp.bfloat16)
            stage_gate[lines, :] = grads[:, :hidden]
            stage_up[lines, :] = grads[:, hidden:]
            stage_down[:, lines] = dot_rows(act[...], sca[q, :, cols]).astype(jnp.bfloat16)
            return carry

        lax.fori_loop(0, width // tile, one, 0)
        for copy in write_copies(q):
            copy.start()

    pack(0)
    recv[0] = send[rank]
    pl.semaphore_wait(barrier, experts + 1)
    dispatch(0, 1)

    for copy in weight_copies:
        copy.wait()

    def turn(t, carry):
        @pl.when(t < ZS)
        def _():
            spread(t)

        def ahead(first, last):
            def one(k, carry):
                pack(k)
                dispatch(k, 0)
                return carry

            lax.fori_loop(first, last, one, 0)

        @pl.when(t == 0)
        def _():
            ahead(1, min(4, ZS))

        @pl.when(t == 1)
        def _():
            ahead(min(4, ZS), min(6, ZS))

        @pl.when((t >= 2) & (t + 4 < ZS))
        def _():
            ahead(t + 4, t + 5)

        @pl.when((t >= 1) & (t < ZS + 1))
        def _():
            onward(t - 1)

        @pl.when((t >= 3) & (t < ZS + 3))
        def _():
            reduce_sides(t - 3)

        @pl.when((t >= 4) & (t < ZS + 4))
        def _():
            go_home(t - 4)

        @pl.when((t >= 2) & (t < ZS + 2))
        def _():
            compute(t - 2)

        @pl.when(t == ZS + 1)
        def _():
            weight_grads(0)

        @pl.when(t == ZS + 2)
        def _():
            weight_grads(1)

        return carry

    lax.fori_loop(0, ZS + 4, turn, 0)
    weight_grads(2)
    weight_grads(3)

    pltpu.make_async_remote_copy(
        src_ref=home_send.at[pl.ds(0, experts - 1)],
        dst_ref=home.at[pl.ds(0, experts - 1)],
        send_sem=home_out.at[0],
        recv_sem=home_sem.at[0],
        device_id=(right, rank),
        device_id_type=MESH,
    ).wait_recv()
    result = jnp.zeros((2 * tok_rows, half), jnp.float32)
    for z in range(ZS):
        block = home[pl.ds(z * plane, plane)].reshape(plane * 2 * CAP, half)
        result += dot_rows(chosen(z, ones, ones), block)
    result = result.astype(jnp.bfloat16)
    out_tokens[:, pl.ds(0, half)] = result[:tok_rows]
    out_tokens[:, pl.ds(half, half)] = result[tok_rows:]

    def finish(k, carry):
        for copy in own_copies(k) + onward_copies(k):
            copy.wait_send()
        for s, side in ((0, right), (1, left)):
            pair_copy(s, k, side).wait_send()
            sum_copy(s, k, side).wait_send()
        return carry

    lax.fori_loop(0, ZS, finish, 0)

    def sent(k, count):
        block_wait(k, count).wait_send()
        pltpu.make_async_remote_copy(
            src_ref=home_send.at[pl.ds(0, count)],
            dst_ref=home.at[pl.ds(0, count)],
            send_sem=home_out.at[k],
            recv_sem=home_sem.at[0],
            device_id=(right, rank),
            device_id_type=MESH,
        ).wait_send()

    sent(0, plane - 1)

    def finish_blocks(k, carry):
        sent(k, plane)
        return carry

    lax.fori_loop(1, ZS, finish_blocks, 0)
    for q in range(PARTS):
        for copy in write_copies(q):
            copy.wait()


def body(tokens, grad_out, route_weights, expert_ids, gate_weight, up_weight, down_weight):
    tok_rows, width = tokens.shape
    experts = lax.axis_size("expert")
    plane = XS * CORES
    rows = plane * CAP
    total = experts * CAP
    features, hidden = gate_weight.shape[1:]
    half = width // 2
    bf16, f32 = jnp.bfloat16, jnp.float32
    vmem, free = pl.BlockSpec(memory_space=pltpu.VMEM), pl.BlockSpec(memory_space=pl.ANY)
    hbm = pl.BlockSpec(memory_space=pltpu.HBM)
    dma = pltpu.SemaphoreType.DMA
    grads = pl.pallas_call(
        kernel,
        out_shape=(
            jax.ShapeDtypeStruct((tok_rows, width), bf16),
            jax.ShapeDtypeStruct((features, hidden), bf16),
            jax.ShapeDtypeStruct((features, hidden), bf16),
            jax.ShapeDtypeStruct((hidden, features), bf16),
        ),
        in_specs=[vmem, vmem, vmem, vmem, hbm, hbm, hbm],
        out_specs=(vmem, free, free, free),
        scratch_shapes=[
            pltpu.VMEM((2 * tok_rows, width), bf16),
            pltpu.VMEM((experts, 2 * CAP, width), bf16),
            pltpu.VMEM((experts, 2 * CAP, width), bf16),
            pltpu.VMEM((PARTS, total, width), bf16),
            pltpu.VMEM((PARTS, total, width), bf16),
            pltpu.VMEM((features, 2 * hidden), bf16),
            pltpu.VMEM((hidden, features), bf16),
            pltpu.VMEM((total, 2 * hidden), bf16),
            pltpu.VMEM((total, hidden), bf16),
            pltpu.VMEM((3, total, width), f32),
            pltpu.VMEM((2, ZS, rows, half), bf16),
            pltpu.VMEM((2, ZS, rows, half), bf16),
            pltpu.VMEM((2, ZS, rows, width), bf16),
            pltpu.VMEM((2, ZS, rows, width), bf16),
            pltpu.VMEM((experts, 2 * CAP, half), bf16),
            pltpu.VMEM((experts, 2 * CAP, half), bf16),
            pltpu.VMEM((features, hidden), bf16),
            pltpu.VMEM((features, hidden), bf16),
            pltpu.VMEM((hidden, features), bf16),
            dma((3,)),
            dma((ZS,)),
            dma((ZS,)),
            dma((4, ZS)),
            dma((2, ZS)),
            dma((6, ZS)),
            dma((2, ZS)),
            dma((2, ZS)),
            dma((2, ZS)),
            dma((2, ZS)),
            dma((ZS,)),
            dma((1,)),
            dma((3, PARTS)),
        ],
        compiler_params=pltpu.CompilerParams(
            collective_id=0, has_side_effects=True, vmem_limit_bytes=44 * 1024 * 1024
        ),
    )(
        expert_ids.T, route_weights.T, tokens, grad_out,
        gate_weight[0], up_weight[0], down_weight[0],
    )
    return (grads[0], grads[1][None], grads[2][None], grads[3][None])


def solution(mesh):
    placed = (
        P("expert", "dp"),
        P("expert", "dp"),
        P("expert", None),
        P("expert", None),
        P("expert", None, "dp"),
        P("expert", None, "dp"),
        P("expert", "dp", None),
    )
    return jax.shard_map(
        body,
        mesh=mesh,
        in_specs=placed,
        out_specs=(
            P("expert", "dp"),
            P("expert", None, "dp"),
            P("expert", None, "dp"),
            P("expert", "dp", None),
        ),
        check_vma=False,
    )
```

```python
import jax
import jax.numpy as jnp
from jax import lax
from jax.experimental import pallas as pl
from jax.experimental.pallas import tpu as pltpu
from jax.sharding import PartitionSpec as P

CAP = 8
PARTS = 4
ZS, XS, CORES = 8, 4, 2
MESH = pl.DeviceIdType.MESH

PLANE_OF = (2, 6, 5, 3, 7, 0, 4, 1)
PLANE_CODE = sum(place << (3 * p) for p, place in enumerate(PLANE_OF))
FAR, NEAR, SAME = 5, 3, 5
SLOTS = 4

SPREAD = (0, 1, 6)
ONWARD = (3, 4, 9)
UNPACK = (8, 9, 12)
COMPUTE = (1, 2, 5, 6, 8, 9, 11, 12)
REDUCE = (4, 5, 8, 10, 11, 12, 13, 15)
GO_HOME = (7, 8, 10, 12, 13, 14, 15, 16)
TURNS = 17


def dot_last(left, right):
    return lax.dot_general(
        left, right, (((1,), (1,)), ((), ())), preferred_element_type=jnp.float32
    )


def dot_rows(left, right):
    return lax.dot_general(
        left, right, (((0,), (0,)), ((), ())), preferred_element_type=jnp.float32
    )


def kernel(
    ids_ref, weights_ref, tokens_ref, grad_ref, gate_hbm, up_hbm, down_hbm,
    out_tokens, out_gate, out_up, out_down,
    dense, far_send, far_recv, near_send, near_recv, tok, sca, wgu, wdn, hid, act, part,
    pair_send, pair_recv, sum_send, sum_recv, home_send, home,
    weight_sems, dense_out, dense_sems, far_out, far_sems, near_out, near_sems,
    own_out, onward_out, row_sems, pair_out, pair_sems, sum_out, sum_sems,
    home_out, home_sem, write_sems,
):
    rank = lax.axis_index("expert")
    y = lax.axis_index("dp")
    plane = XS * CORES
    experts = ZS * plane
    rows = plane * CAP
    zi, xi, ci = rank // plane, (rank // CORES) % XS, rank % CORES
    right, left = (y + 1) % PARTS, (y + PARTS - 1) % PARTS
    across = (y + 2) % PARTS
    tok_rows, width = tokens_ref.shape
    half = width // 2
    hidden = act.shape[1]

    def at(row, col):
        return pl.ds(pl.multiple_of(row * col, col), col)

    def offset(p):
        return (PLANE_CODE >> (3 * p)) % 8

    def far_block(j):
        return j + 2 * (j // 4)

    def near_block(n):
        return 4 + n + n // 2

    def peer(p, i, sign):
        z = (zi + sign * offset(p) + ZS) % ZS
        x = (xi + sign * (i // CORES) + XS) % XS
        c = (ci + i) % CORES
        return z * plane + x * CORES + c

    def remote(src, dst, out, arrive, device):
        return pltpu.make_async_remote_copy(
            src_ref=src, dst_ref=dst, send_sem=out, recv_sem=arrive,
            device_id=device, device_id_type=MESH,
        )

    barrier = pltpu.get_barrier_semaphore()

    def greet(j, carry):
        pl.semaphore_signal(
            barrier, inc=1, device_id=(y, (rank + j) % experts), device_id_type=MESH
        )
        return carry

    lax.fori_loop(1, experts, greet, 0)
    for side in (left, right):
        pl.semaphore_signal(barrier, inc=1, device_id=(side, rank), device_id_type=MESH)

    weight_copies = [
        pltpu.make_async_copy(gate_hbm, wgu.at[:, pl.ds(0, hidden)], weight_sems.at[0]),
        pltpu.make_async_copy(up_hbm, wgu.at[:, pl.ds(hidden, hidden)], weight_sems.at[1]),
        pltpu.make_async_copy(down_hbm, wdn, weight_sems.at[2]),
    ]
    for copy in weight_copies:
        copy.start()

    dense[y, pl.ds(0, tok_rows), :] = tokens_ref[...]
    dense[y, pl.ds(tok_rows, tok_rows), :] = grad_ref[...]

    def dense_copy(h, q, out, arrive, side):
        block = dense.at[q, pl.ds(h * tok_rows, tok_rows)]
        return remote(block, block, out, dense_sems.at[arrive], (side, rank))

    def dense_own():
        return [
            dense_copy(0, y, dense_out.at[0], 0, right),
            dense_copy(1, y, dense_out.at[1], 3, left),
            dense_copy(1, y, dense_out.at[2], 1, right),
            dense_copy(0, y, dense_out.at[3], 2, left),
        ]

    def dense_onward():
        return [
            dense_copy(0, left, dense_out.at[4], 4, right),
            dense_copy(1, right, dense_out.at[5], 5, left),
        ]

    def dense_arrival(h, q, arrive):
        dense_copy(h, q, dense_out.at[0], arrive, right).wait_recv()

    ids, weights = ids_ref[...], weights_ref[...].astype(jnp.float32)
    numbers = lax.broadcasted_iota(jnp.int32, (experts, tok_rows), 0)
    hits = [numbers == ids[c : c + 1] for c in range(2)]
    before = lax.broadcasted_iota(jnp.int32, (tok_rows, tok_rows), 0) < (
        lax.broadcasted_iota(jnp.int32, (tok_rows, tok_rows), 1)
    )
    earlier = jnp.dot(
        jnp.where(hits[0] | hits[1], 1.0, 0.0).astype(jnp.bfloat16),
        jnp.where(before, 1.0, 0.0).astype(jnp.bfloat16),
        preferred_element_type=jnp.float32,
    )
    place = [
        jnp.sum(jnp.where(hits[c], earlier, 0.0), axis=0, keepdims=True)
        + ids[c : c + 1].astype(jnp.float32) * (2 * CAP)
        for c in range(2)
    ]

    def chosen(z, first, second):
        line = lax.broadcasted_iota(jnp.int32, (plane * 2 * CAP, tok_rows), 0)
        line = (line + z * (plane * 2 * CAP)).astype(jnp.float32)
        halves = [
            jnp.where(line == place[0] + shift, value[0:1], 0.0)
            + jnp.where(line == place[1] + shift, value[1:2], 0.0)
            for shift, value in ((0.0, first), (float(CAP), second))
        ]
        return jnp.concatenate(halves, axis=1).astype(jnp.bfloat16)

    ones = jnp.ones_like(weights)

    def picks(p):
        return chosen((zi - offset(p) + ZS) % ZS, ones, weights)

    def pick(which, q):
        picked = jnp.dot(which, dense[q], preferred_element_type=jnp.float32)
        return picked.astype(jnp.bfloat16).reshape(plane, 2 * CAP, width)

    def far_copy(j, i):
        target = peer(far_block(j), i, -1)
        return remote(
            far_send.at[j, target % plane], far_recv.at[j, i],
            far_out.at[j], far_sems.at[j], (y, target),
        )

    def far_whole(j):
        return remote(far_send.at[j], far_recv.at[j], far_out.at[j], far_sems.at[j], (right, rank))

    def pack_far(j):
        far_send[j] = pick(picks(far_block(j)), y)

    def dispatch_far(j, carry):
        def one(i, inner):
            far_copy(j, i).start()
            return inner

        return lax.fori_loop(0, plane, one, carry)

    def near_copy(n, i):
        target = peer(near_block(n), i, -1)
        return remote(
            near_send.at[n, target % plane], near_recv.at[n, i],
            near_out.at[n], near_sems.at[n], (y, target),
        )

    def near_whole(n, first):
        some = pl.ds(first, plane - first)
        return remote(
            near_send.at[n, some], near_recv.at[n, some],
            near_out.at[n], near_sems.at[n], (right, rank),
        )

    def dispatch_near(n, carry):
        which = picks(near_block(n))
        for q in range(PARTS):
            near_send[n, :, q] = pick(which, q)

        def one(i, inner):
            near_copy(n, i).start()
            return inner

        same = near_block(n) == SAME

        @pl.when(same)
        def _():
            near_recv[n, 0] = near_send[n, rank % plane]
            lax.fori_loop(1, plane, one, 0)

        @pl.when(jnp.logical_not(same))
        def _():
            lax.fori_loop(0, plane, one, 0)

        return carry

    def side_copy(buf, q, p, out, arrive, side):
        block = buf.at[q, at(p, rows)]
        return remote(block, block, out, arrive, (side, rank))

    def own_copies(j):
        p = far_block(j)
        return [
            side_copy(tok, y, p, own_out.at[0, j], row_sems.at[0, j], right),
            side_copy(sca, y, p, own_out.at[1, j], row_sems.at[3, j], left),
            side_copy(sca, y, p, own_out.at[2, j], row_sems.at[1, j], right),
            side_copy(tok, y, p, own_out.at[3, j], row_sems.at[2, j], left),
        ]

    def onward_copies(j):
        p = far_block(j)
        return [
            side_copy(tok, left, p, onward_out.at[0, j], row_sems.at[4, j], right),
            side_copy(sca, right, p, onward_out.at[1, j], row_sems.at[5, j], left),
        ]

    def arrival(buf, q, j, arrive):
        side_copy(
            buf, q, far_block(j), own_out.at[0, j], row_sems.at[arrive, j], right
        ).wait_recv()

    def separate(got, q, p):
        got = got.astype(jnp.float32)
        mine = at(p, rows)
        tok[q, mine, :] = got[:, :CAP, :].reshape(rows, width).astype(jnp.bfloat16)
        sca[q, mine, :] = got[:, CAP:, :].reshape(rows, width).astype(jnp.bfloat16)

    def spread(j):
        far_whole(j).wait_recv()
        separate(far_recv[j], y, far_block(j))
        for copy in own_copies(j):
            copy.start()

    def onward(j):
        copies = onward_copies(j)
        arrival(tok, left, j, 0)
        copies[0].start()
        arrival(sca, right, j, 3)
        copies[1].start()

    def unpack(n):
        p = near_block(n)

        @pl.when(p == SAME)
        def _():
            near_whole(n, 1).wait_recv()

        @pl.when(p != SAME)
        def _():
            near_whole(n, 0).wait_recv()

        for q in range(PARTS):
            separate(near_recv[n, :, q], q, p)

    def pair_copy(s, p, side):
        return remote(
            pair_send.at[s, p], pair_recv.at[s, p], pair_out.at[s, p], pair_sems.at[s, p],
            (side, rank),
        )

    def sum_copy(s, p, side):
        return remote(
            sum_send.at[s, p], sum_recv.at[s, p], sum_out.at[s, p], sum_sems.at[s, p],
            (side, rank),
        )

    def compute(p):
        mine = at(p, rows)

        @pl.when((p < 4) | (p == 6))
        def _():
            j = p - 2 * (p // 6)
            arrival(sca, left, j, 1)
            arrival(tok, right, j, 2)
            arrival(tok, across, j, 4)
            arrival(sca, across, j, 5)

        pre = jnp.zeros((rows, 2 * hidden), jnp.float32)
        grad_act = jnp.zeros((rows, hidden), jnp.float32)
        for q in range(PARTS):
            pre += jnp.dot(
                tok[q, mine, :], wgu[pl.ds(q * width, width), :],
                preferred_element_type=jnp.float32,
            )
            grad_act += dot_last(sca[q, mine, :], wdn[:, pl.ds(q * width, width)])
        gate_pre, up_pre = pre[:, :hidden], pre[:, hidden:]
        sigmoid_gate = 1.0 / (1.0 + jnp.exp(-gate_pre))
        swish_gate = gate_pre * sigmoid_gate
        act[mine, :] = (swish_gate * up_pre).astype(jnp.bfloat16)
        hid[mine, :] = jnp.concatenate(
            [
                grad_act * up_pre * sigmoid_gate * (1.0 + gate_pre * (1.0 - sigmoid_gate)),
                grad_act * swish_gate,
            ],
            axis=1,
        ).astype(jnp.bfloat16)

        def back(q):
            return dot_last(hid[mine, :], wgu[at(q, width), :])

        far = back(across).astype(jnp.bfloat16)
        pair_send[0, p] = far[:, :half]
        pair_send[1, p] = far[:, half:]
        pair_copy(0, p, right).start()
        pair_copy(1, p, left).start()
        slot = p % SLOTS
        part[slot, 0] = back(right)
        part[slot, 1] = back(left)
        part[slot, 2] = back(y)

    def reduce_sides(p):
        slot = p % SLOTS
        pair_copy(0, p, right).wait_recv()
        near = part[slot, 0]
        sum_send[0, p] = jnp.concatenate(
            [near[:, :half] + pair_recv[0, p].astype(jnp.float32), near[:, half:]], axis=1
        ).astype(jnp.bfloat16)
        sum_copy(0, p, right).start()
        pair_copy(1, p, left).wait_recv()
        near = part[slot, 1]
        sum_send[1, p] = jnp.concatenate(
            [near[:, :half], near[:, half:] + pair_recv[1, p].astype(jnp.float32)], axis=1
        ).astype(jnp.bfloat16)
        sum_copy(1, p, left).start()

    def home_copy(p, i):
        return remote(
            home_send.at[p * plane + i], home.at[rank], home_out.at[p], home_sem.at[0],
            (y, peer(p, i, 1)),
        )

    def go_home(p):
        sum_copy(0, p, right).wait_recv()
        sum_copy(1, p, left).wait_recv()
        total = (
            part[p % SLOTS, 2]
            + sum_recv[0, p].astype(jnp.float32)
            + sum_recv[1, p].astype(jnp.float32)
        ).reshape(plane, CAP, width)
        home_send[at(p, plane)] = jnp.concatenate(
            [total[:, :, :half], total[:, :, half:]], axis=1
        ).astype(jnp.bfloat16)

        def one(i, carry):
            home_copy(p, i).start()
            return carry

        @pl.when(p == SAME)
        def _():
            home[rank] = home_send[SAME * plane]
            lax.fori_loop(1, plane, one, 0)

        @pl.when(p != SAME)
        def _():
            lax.fori_loop(0, plane, one, 0)

    def write_copies(q):
        lines = pl.ds(q * width, width)
        return [
            pltpu.make_async_copy(
                wgu.at[lines, pl.ds(0, hidden)], out_gate.at[lines], write_sems.at[0, q]
            ),
            pltpu.make_async_copy(
                wgu.at[lines, pl.ds(hidden, hidden)], out_up.at[lines], write_sems.at[1, q]
            ),
            pltpu.make_async_copy(wdn.at[:, lines], out_down.at[:, lines], write_sems.at[2, q]),
        ]

    def weight_grads(q):
        tile = min(256, width)

        def one(j, carry):
            cols = at(j, tile)
            lines = pl.ds(pl.multiple_of(q * width + j * tile, tile), tile)
            wgu[lines, :] = dot_rows(tok[q, :, cols], hid[...]).astype(jnp.bfloat16)
            wdn[:, lines] = dot_rows(act[...], sca[q, :, cols]).astype(jnp.bfloat16)
            return carry

        lax.fori_loop(0, width // tile, one, 0)
        for copy in write_copies(q):
            copy.start()

    pack_far(0)
    pl.semaphore_wait(barrier, experts + 1)
    for copy in dense_own():
        copy.start()
    dispatch_far(0, 0)

    def next_far(j, carry):
        pack_far(j)
        return dispatch_far(j, carry)

    lax.fori_loop(1, 3, next_far, 0)
    copies = dense_onward()
    dense_arrival(0, left, 0)
    copies[0].start()
    dense_arrival(1, right, 3)
    copies[1].start()
    lax.fori_loop(3, FAR, next_far, 0)
    for copy in weight_copies:
        copy.wait()

    def next_spread(j, carry):
        spread(j)
        return carry

    def next_onward(j, carry):
        onward(j)
        return carry

    lax.fori_loop(0, 2, next_spread, 0)
    dense_arrival(1, left, 1)
    dense_arrival(0, right, 2)
    dense_arrival(0, across, 4)
    dense_arrival(1, across, 5)
    lax.fori_loop(0, NEAR, dispatch_near, 0)
    lax.fori_loop(0, 2, next_onward, 0)

    def turn(t, carry):
        def stage(turns, work, done):
            now = t == turns[0]
            for at_turn in turns[1:]:
                now = now | (t == at_turn)

            @pl.when(now)
            def _():
                index = done
                for at_turn in turns:
                    index = index + jnp.where(t > at_turn, 1, 0)
                work(index)

        stage(ONWARD, onward, 2)
        stage(REDUCE, reduce_sides, 0)
        stage(GO_HOME, go_home, 0)
        stage(SPREAD, spread, 2)
        stage(UNPACK, unpack, 0)
        stage(COMPUTE, compute, 0)
        return carry

    lax.fori_loop(0, TURNS, turn, 0)
    for q in range(PARTS):
        weight_grads(q)

    remote(
        home_send.at[pl.ds(0, experts - 1)], home.at[pl.ds(0, experts - 1)],
        home_out.at[0], home_sem.at[0], (right, rank),
    ).wait_recv()
    result = jnp.zeros((2 * tok_rows, half), jnp.float32)
    for z in range(ZS):
        block = home[pl.ds(z * plane, plane)].reshape(plane * 2 * CAP, half)
        result += dot_rows(chosen(z, ones, ones), block)
    result = result.astype(jnp.bfloat16)
    out_tokens[:, pl.ds(0, half)] = result[:tok_rows]
    out_tokens[:, pl.ds(half, half)] = result[tok_rows:]

    for copy in dense_own() + dense_onward():
        copy.wait_send()

    def finish_far(j, carry):
        far_whole(j).wait_send()
        for copy in own_copies(j) + onward_copies(j):
            copy.wait_send()
        return carry

    lax.fori_loop(0, FAR, finish_far, 0)
    for n in range(NEAR):
        near_whole(n, 1 if near_block(n) == SAME else 0).wait_send()

    def home_sent(p, count):
        some = pl.ds(0, count)
        remote(
            home_send.at[some], home.at[some], home_out.at[p], home_sem.at[0], (right, rank)
        ).wait_send()

    def finish(p, carry):
        for s, side in ((0, right), (1, left)):
            pair_copy(s, p, side).wait_send()
            sum_copy(s, p, side).wait_send()

        @pl.when(p == SAME)
        def _():
            home_sent(p, plane - 1)

        @pl.when(p != SAME)
        def _():
            home_sent(p, plane)

        return carry

    lax.fori_loop(0, ZS, finish, 0)
    for q in range(PARTS):
        for copy in write_copies(q):
            copy.wait()


def body(tokens, grad_out, route_weights, expert_ids, gate_weight, up_weight, down_weight):
    tok_rows, width = tokens.shape
    experts = lax.axis_size("expert")
    plane = XS * CORES
    rows = plane * CAP
    total = experts * CAP
    features, hidden = gate_weight.shape[1:]
    half = width // 2
    bf16, f32 = jnp.bfloat16, jnp.float32
    vmem, free = pl.BlockSpec(memory_space=pltpu.VMEM), pl.BlockSpec(memory_space=pl.ANY)
    hbm = pl.BlockSpec(memory_space=pltpu.HBM)
    dma = pltpu.SemaphoreType.DMA
    grads = pl.pallas_call(
        kernel,
        out_shape=(
            jax.ShapeDtypeStruct((tok_rows, width), bf16),
            jax.ShapeDtypeStruct((features, hidden), bf16),
            jax.ShapeDtypeStruct((features, hidden), bf16),
            jax.ShapeDtypeStruct((hidden, features), bf16),
        ),
        in_specs=[vmem, vmem, vmem, vmem, hbm, hbm, hbm],
        out_specs=(vmem, free, free, free),
        scratch_shapes=[
            pltpu.VMEM((PARTS, 2 * tok_rows, width), bf16),
            pltpu.VMEM((FAR, plane, 2 * CAP, width), bf16),
            pltpu.VMEM((FAR, plane, 2 * CAP, width), bf16),
            pltpu.VMEM((NEAR, plane, PARTS, 2 * CAP, width), bf16),
            pltpu.VMEM((NEAR, plane, PARTS, 2 * CAP, width), bf16),
            pltpu.VMEM((PARTS, total, width), bf16),
            pltpu.VMEM((PARTS, total, width), bf16),
            pltpu.VMEM((features, 2 * hidden), bf16),
            pltpu.VMEM((hidden, features), bf16),
            pltpu.VMEM((total, 2 * hidden), bf16),
            pltpu.VMEM((total, hidden), bf16),
            pltpu.VMEM((SLOTS, 3, rows, width), f32),
            pltpu.VMEM((2, ZS, rows, half), bf16),
            pltpu.VMEM((2, ZS, rows, half), bf16),
            pltpu.VMEM((2, ZS, rows, width), bf16),
            pltpu.VMEM((2, ZS, rows, width), bf16),
            pltpu.VMEM((experts, 2 * CAP, half), bf16),
            pltpu.VMEM((experts, 2 * CAP, half), bf16),
            dma((3,)),
            dma((6,)),
            dma((6,)),
            dma((FAR,)),
            dma((FAR,)),
            dma((NEAR,)),
            dma((NEAR,)),
            dma((4, FAR)),
            dma((2, FAR)),
            dma((6, FAR)),
            dma((2, ZS)),
            dma((2, ZS)),
            dma((2, ZS)),
            dma((2, ZS)),
            dma((ZS,)),
            dma((1,)),
            dma((3, PARTS)),
        ],
        compiler_params=pltpu.CompilerParams(
            collective_id=0, has_side_effects=True, vmem_limit_bytes=47 * 1024 * 1024
        ),
    )(
        expert_ids.T, route_weights.T, tokens, grad_out,
        gate_weight[0], up_weight[0], down_weight[0],
    )
    return (grads[0], grads[1][None], grads[2][None], grads[3][None])


def solution(mesh):
    placed = (
        P("expert", "dp"),
        P("expert", "dp"),
        P("expert", None),
        P("expert", None),
        P("expert", None, "dp"),
        P("expert", None, "dp"),
        P("expert", "dp", None),
    )
    return jax.shard_map(
        body,
        mesh=mesh,
        in_specs=placed,
        out_specs=(
            P("expert", "dp"),
            P("expert", None, "dp"),
            P("expert", None, "dp"),
            P("expert", "dp", None),
        ),
        check_vma=False,
    )
```

```python
import jax
import jax.numpy as jnp
from jax import lax
from jax.experimental import pallas as pl
from jax.experimental.pallas import tpu as pltpu
from jax.sharding import PartitionSpec as P

CAP = 8
PARTS = 4
ZS, XS, CORES = 8, 4, 2
MESH = pl.DeviceIdType.MESH

PLANE_OF = (5, 3, 2, 6, 0, 4, 7, 1)
FAR, NEAR, SAME = 5, 3, 4
SLOTS = 6


def code(items):
    return sum(item << (3 * place) for place, item in enumerate(items))


PLANE_CODE = code(PLANE_OF)

GATHER_DONE = ((2,), (4,))
SEND_NEAR = ((2, 4, 6), (0, 1, 2))
ONWARD = ((2, 3, 6, 7, 8), (3, 1, 0, 2, 4))
SPREAD = ((0, 1, 4, 5, 7), (3, 1, 0, 2, 4))
UNPACK = ((7, 11, 12), (0, 2, 1))
COMPUTE = ((7, 8, 10, 15), (0, 1, 2, 3))
REDUCE = ((8, 9, 10, 12, 13, 14, 17, 18), (1, 0, 2, 5, 4, 3, 6, 7))
GO_HOME = ((10, 11, 14, 15, 16, 19, 20, 21), (1, 0, 2, 5, 3, 6, 4, 7))
WEIGHTS = ((17, 18), (0, 1))
TURNS = 22


def dot_last(left, right):
    return lax.dot_general(
        left, right, (((1,), (1,)), ((), ())), preferred_element_type=jnp.float32
    )


def dot_rows(left, right):
    return lax.dot_general(
        left, right, (((0,), (0,)), ((), ())), preferred_element_type=jnp.float32
    )


def kernel(
    table_ref, both_ref, gate_hbm, up_hbm, down_hbm,
    out_tokens, out_gate, out_up, out_down,
    dense, far_send, far_recv, near_send, near_recv, tok, sca, wgu, wdn, hid, act, act_turned, part,
    pair_send, pair_recv, sum_send, sum_recv, home_send, home,
    weight_sems, dense_out, dense_sems, far_out, far_sems, near_out, near_sems,
    own_out, onward_out, row_sems, pair_out, pair_sems, sum_out, sum_sems,
    home_out, home_sems, write_sems,
):
    rank = lax.axis_index("expert")
    y = lax.axis_index("dp")
    plane = XS * CORES
    experts = ZS * plane
    rows = plane * CAP
    zi, xi, ci = rank // plane, (rank // CORES) % XS, rank % CORES
    right, left = (y + 1) % PARTS, (y + PARTS - 1) % PARTS
    across = (y + 2) % PARTS
    tok_rows, width = both_ref.shape[0] // 2, both_ref.shape[1]
    half = width // 2
    hidden = act.shape[1]

    def at(row, col):
        return pl.ds(pl.multiple_of(row * col, col), col)

    def offset(p):
        return (PLANE_CODE >> (3 * p)) % 8

    def far_block(j):
        return j + j // 4

    def near_block(n):
        return 4 + n + (n + 1) // 2

    def peer(p, i, sign):
        z = (zi + sign * offset(p) + ZS) % ZS
        x = (xi + sign * (i // CORES) + XS) % XS
        c = (ci + i) % CORES
        return z * plane + x * CORES + c

    def remote(src, dst, out, arrive, device):
        return pltpu.make_async_remote_copy(
            src_ref=src, dst_ref=dst, send_sem=out, recv_sem=arrive,
            device_id=device, device_id_type=MESH,
        )

    barrier = pltpu.get_barrier_semaphore()

    def greet(j, carry):
        pl.semaphore_signal(
            barrier, inc=1, device_id=(y, (rank + j) % experts), device_id_type=MESH
        )
        return carry

    lax.fori_loop(1, experts, greet, 0)
    for side in (left, right):
        pl.semaphore_signal(barrier, inc=1, device_id=(side, rank), device_id_type=MESH)

    weight_copies = [
        pltpu.make_async_copy(gate_hbm, wgu.at[:, pl.ds(0, hidden)], weight_sems.at[0]),
        pltpu.make_async_copy(up_hbm, wgu.at[:, pl.ds(hidden, hidden)], weight_sems.at[1]),
        pltpu.make_async_copy(down_hbm, wdn, weight_sems.at[2]),
    ]
    for copy in weight_copies:
        copy.start()

    dense[y] = both_ref[...]

    def dense_copy(h, q, out, arrive, side):
        block = dense.at[q, pl.ds(h * tok_rows, tok_rows)]
        return remote(block, block, out, dense_sems.at[arrive], (side, rank))

    def dense_own():
        return [
            dense_copy(0, y, dense_out.at[0], 0, right),
            dense_copy(1, y, dense_out.at[1], 3, left),
            dense_copy(1, y, dense_out.at[2], 1, right),
            dense_copy(0, y, dense_out.at[3], 2, left),
        ]

    def dense_onward():
        return [
            dense_copy(0, left, dense_out.at[4], 4, right),
            dense_copy(1, right, dense_out.at[5], 5, left),
        ]

    def dense_arrival(h, q, arrive):
        dense_copy(h, q, dense_out.at[0], arrive, right).wait_recv()

    ids, weights = table_ref[0:2], table_ref[2:4]
    numbers = lax.broadcasted_iota(jnp.int32, (experts, tok_rows), 0).astype(jnp.float32)
    hits = [numbers == ids[c : c + 1] for c in range(2)]
    before = lax.broadcasted_iota(jnp.int32, (tok_rows, tok_rows), 0) < (
        lax.broadcasted_iota(jnp.int32, (tok_rows, tok_rows), 1)
    )
    earlier = jnp.dot(
        jnp.where(hits[0] | hits[1], 1.0, 0.0).astype(jnp.bfloat16),
        jnp.where(before, 1.0, 0.0).astype(jnp.bfloat16),
        preferred_element_type=jnp.float32,
    )
    place = [
        jnp.sum(jnp.where(hits[c], earlier, 0.0), axis=0, keepdims=True)
        + ids[c : c + 1] * (2 * CAP)
        for c in range(2)
    ]

    def chosen(z, first, second):
        line = lax.broadcasted_iota(jnp.int32, (plane * 2 * CAP, tok_rows), 0)
        line = (line + z * (plane * 2 * CAP)).astype(jnp.float32)
        halves = [
            jnp.where(line == place[0] + shift, value[0:1], 0.0)
            + jnp.where(line == place[1] + shift, value[1:2], 0.0)
            for shift, value in ((0.0, first), (float(CAP), second))
        ]
        return jnp.concatenate(halves, axis=1).astype(jnp.bfloat16)

    ones = jnp.ones_like(weights)

    def picks(p):
        return chosen((zi - offset(p) + ZS) % ZS, ones, weights)

    def pick(which, q):
        picked = jnp.dot(which, dense[q], preferred_element_type=jnp.float32)
        return picked.astype(jnp.bfloat16).reshape(plane, 2 * CAP, width)

    def far_copy(j, i):
        target = peer(far_block(j), i, -1)
        return remote(
            far_send.at[j, target % plane], far_recv.at[j, i],
            far_out.at[j], far_sems.at[j], (y, target),
        )

    def far_whole(j):
        return remote(far_send.at[j], far_recv.at[j], far_out.at[j], far_sems.at[j], (right, rank))

    def pack_far(j):
        far_send[j] = pick(picks(far_block(j)), y)

    def dispatch_far(j, carry):
        def one(i, inner):
            far_copy(j, i).start()
            return inner

        return lax.fori_loop(0, plane, one, carry)

    def near_copy(n, i):
        target = peer(near_block(n), i, -1)
        return remote(
            near_send.at[n, target % plane], near_recv.at[n, i],
            near_out.at[n], near_sems.at[n], (y, target),
        )

    def near_whole(n, first):
        some = pl.ds(first, plane - first)
        return remote(
            near_send.at[n, some], near_recv.at[n, some],
            near_out.at[n], near_sems.at[n], (right, rank),
        )

    def dispatch_near(n):
        which = picks(near_block(n))
        for q in range(PARTS):
            near_send[n, :, q] = pick(which, q)

        def one(i, inner):
            near_copy(n, i).start()
            return inner

        same = near_block(n) == SAME

        @pl.when(same)
        def _():
            near_recv[n, 0] = near_send[n, rank % plane]
            lax.fori_loop(1, plane, one, 0)

        @pl.when(jnp.logical_not(same))
        def _():
            lax.fori_loop(0, plane, one, 0)

    def side_copy(buf, q, p, out, arrive, side):
        block = buf.at[q, at(p, rows)]
        return remote(block, block, out, arrive, (side, rank))

    def own_copies(j):
        p = far_block(j)
        return [
            side_copy(tok, y, p, own_out.at[0, j], row_sems.at[0, j], right),
            side_copy(sca, y, p, own_out.at[1, j], row_sems.at[3, j], left),
            side_copy(sca, y, p, own_out.at[2, j], row_sems.at[1, j], right),
            side_copy(tok, y, p, own_out.at[3, j], row_sems.at[2, j], left),
        ]

    def onward_copies(j):
        p = far_block(j)
        return [
            side_copy(tok, left, p, onward_out.at[0, j], row_sems.at[4, j], right),
            side_copy(sca, right, p, onward_out.at[1, j], row_sems.at[5, j], left),
        ]

    def arrival(buf, q, j, arrive):
        side_copy(
            buf, q, far_block(j), own_out.at[0, j], row_sems.at[arrive, j], right
        ).wait_recv()

    def separate(got, q, p):
        got = got.astype(jnp.float32)
        mine = at(p, rows)
        tok[q, mine, :] = got[:, :CAP, :].reshape(rows, width).astype(jnp.bfloat16)
        sca[q, mine, :] = got[:, CAP:, :].reshape(rows, width).astype(jnp.bfloat16)

    def spread(j):
        far_whole(j).wait_recv()
        separate(far_recv[j], y, far_block(j))
        for copy in own_copies(j):
            copy.start()

    def onward(j):
        copies = onward_copies(j)
        arrival(tok, left, j, 0)
        copies[0].start()
        arrival(sca, right, j, 3)
        copies[1].start()

    def unpack(n):
        p = near_block(n)

        @pl.when(p == SAME)
        def _():
            near_whole(n, 1).wait_recv()

        @pl.when(p != SAME)
        def _():
            near_whole(n, 0).wait_recv()

        for q in range(PARTS):
            separate(near_recv[n, :, q], q, p)

    def pair_copy(s, p, side):
        return remote(
            pair_send.at[s, p], pair_recv.at[s, p], pair_out.at[s, p], pair_sems.at[s, p],
            (side, rank),
        )

    def sum_copy(s, p, side):
        return remote(
            sum_send.at[s, p], sum_recv.at[s, p], sum_out.at[s, p], sum_sems.at[s, p],
            (side, rank),
        )

    def compute(pair):
        mine = at(pair, 2 * rows)

        def gathered(j):
            arrival(sca, left, j, 1)
            arrival(tok, right, j, 2)
            arrival(tok, across, j, 4)
            arrival(sca, across, j, 5)

        @pl.when(pair < 2)
        def _():
            gathered(2 * pair)
            gathered(2 * pair + 1)

        @pl.when(pair == 2)
        def _():
            gathered(4)

        pre = jnp.zeros((2 * rows, 2 * hidden), jnp.float32)
        grad_act = jnp.zeros((2 * rows, hidden), jnp.float32)
        for q in range(PARTS):
            pre += jnp.dot(
                tok[q, mine, :], wgu[pl.ds(q * width, width), :],
                preferred_element_type=jnp.float32,
            )
            grad_act += dot_last(sca[q, mine, :], wdn[:, pl.ds(q * width, width)])
        gate_pre, up_pre = pre[:, :hidden], pre[:, hidden:]
        sigmoid_gate = 1.0 / (1.0 + jnp.exp(-gate_pre))
        swish_gate = gate_pre * sigmoid_gate
        act[mine, :] = (swish_gate * up_pre).astype(jnp.bfloat16)
        hid[mine, :] = jnp.concatenate(
            [
                grad_act * up_pre * sigmoid_gate * (1.0 + gate_pre * (1.0 - sigmoid_gate)),
                grad_act * swish_gate,
            ],
            axis=1,
        ).astype(jnp.bfloat16)

        def back(q):
            return dot_last(hid[mine, :], wgu[at(q, width), :])

        far = back(across).astype(jnp.bfloat16)
        for i in range(2):
            p = 2 * pair + i
            pair_send[0, p] = far[i * rows : (i + 1) * rows, :half]
            pair_send[1, p] = far[i * rows : (i + 1) * rows, half:]
            pair_copy(0, p, right).start()
            pair_copy(1, p, left).start()
        for kept, q in enumerate((right, left, y)):
            mine_part = back(q)
            for i in range(2):
                part[(2 * pair + i) % SLOTS, kept] = mine_part[i * rows : (i + 1) * rows]

    def reduce_sides(p):
        slot = p % SLOTS
        pair_copy(0, p, right).wait_recv()
        near = part[slot, 0]
        sum_send[0, p] = jnp.concatenate(
            [near[:, :half] + pair_recv[0, p].astype(jnp.float32), near[:, half:]], axis=1
        ).astype(jnp.bfloat16)
        sum_copy(0, p, right).start()
        pair_copy(1, p, left).wait_recv()
        near = part[slot, 1]
        sum_send[1, p] = jnp.concatenate(
            [near[:, :half], near[:, half:] + pair_recv[1, p].astype(jnp.float32)], axis=1
        ).astype(jnp.bfloat16)
        sum_copy(1, p, left).start()

    def home_copy(p, i):
        return remote(
            home_send.at[p * plane + i], home.at[rank], home_out.at[p], home_sems.at[p],
            (y, peer(p, i, 1)),
        )

    def go_home(p):
        sum_copy(0, p, right).wait_recv()
        sum_copy(1, p, left).wait_recv()
        total = (
            part[p % SLOTS, 2]
            + sum_recv[0, p].astype(jnp.float32)
            + sum_recv[1, p].astype(jnp.float32)
        ).reshape(plane, CAP, width)
        home_send[at(p, plane)] = jnp.concatenate(
            [total[:, :, :half], total[:, :, half:]], axis=1
        ).astype(jnp.bfloat16)

        def one(i, carry):
            home_copy(p, i).start()
            return carry

        @pl.when(p == SAME)
        def _():
            home[rank] = home_send[SAME * plane]
            lax.fori_loop(1, plane, one, 0)

        @pl.when(p != SAME)
        def _():
            lax.fori_loop(0, plane, one, 0)

    def write_copies(q):
        lines = at(q, width)
        return [
            pltpu.make_async_copy(
                wgu.at[lines, pl.ds(0, hidden)], out_gate.at[lines], write_sems.at[0, q]
            ),
            pltpu.make_async_copy(
                wgu.at[lines, pl.ds(hidden, hidden)], out_up.at[lines], write_sems.at[1, q]
            ),
            pltpu.make_async_copy(wdn.at[:, lines], out_down.at[:, lines], write_sems.at[2, q]),
        ]

    def weight_grads(q):
        tile = min(256, width)

        def turned(block):
            size = block.shape[1]
            diagonal = lax.broadcasted_iota(jnp.int32, (size, size), 0) == (
                lax.broadcasted_iota(jnp.int32, (size, size), 1)
            )
            unit = jnp.where(diagonal, 1.0, 0.0).astype(jnp.bfloat16)
            return dot_last(unit, block).astype(jnp.bfloat16)

        @pl.when(q == 0)
        def _():
            act_turned[...] = turned(act[...])

        def one(j, carry):
            cols = at(j, tile)
            lines = pl.ds(pl.multiple_of(q * width + j * tile, tile), tile)
            wgu[lines, :] = jnp.dot(
                turned(tok[q, :, cols]), hid[...], preferred_element_type=jnp.float32
            ).astype(jnp.bfloat16)
            wdn[:, lines] = jnp.dot(
                act_turned[...], sca[q, :, cols], preferred_element_type=jnp.float32
            ).astype(jnp.bfloat16)
            return carry

        lax.fori_loop(0, width // tile, one, 0)
        for copy in write_copies(q):
            copy.start()

    def next_far(j, carry):
        pack_far(j)
        return dispatch_far(j, carry)

    pack_far(1)
    pl.semaphore_wait(barrier, experts + 1)
    for copy in dense_own():
        copy.start()
    dispatch_far(1, 0)
    lax.fori_loop(2, 4, next_far, 0)
    copies = dense_onward()
    dense_arrival(0, left, 0)
    copies[0].start()
    dense_arrival(1, right, 3)
    copies[1].start()
    next_far(0, 0)
    for copy in weight_copies:
        copy.wait()

    def gather_done(j):
        dense_arrival(1, left, 1)
        dense_arrival(0, right, 2)
        dense_arrival(0, across, 4)
        dense_arrival(1, across, 5)
        next_far(j, 0)

    def turn(t, carry):
        def stage(plan, work):
            turns, blocks = plan
            now = t == turns[0]
            for at_turn in turns[1:]:
                now = now | (t == at_turn)

            @pl.when(now)
            def _():
                index = 0
                for at_turn in turns:
                    index = index + jnp.where(t > at_turn, 1, 0)
                work((code(blocks) >> (3 * index)) % 8)

        stage(GATHER_DONE, gather_done)
        stage(SEND_NEAR, dispatch_near)
        stage(ONWARD, onward)
        stage(SPREAD, spread)
        stage(UNPACK, unpack)
        stage(COMPUTE, compute)
        stage(REDUCE, reduce_sides)
        stage(GO_HOME, go_home)
        stage(WEIGHTS, weight_grads)
        return carry

    lax.fori_loop(0, TURNS, turn, 0)
    for q in range(len(WEIGHTS[0]), PARTS):
        weight_grads(q)

    for copy in dense_own() + dense_onward():
        copy.wait_send()

    def finish_far(j, carry):
        far_whole(j).wait_send()
        for copy in own_copies(j) + onward_copies(j):
            copy.wait_send()
        return carry

    lax.fori_loop(0, FAR, finish_far, 0)
    for n in range(NEAR):
        near_whole(n, 1 if near_block(n) == SAME else 0).wait_send()

    def finish_sides(p, carry):
        for s, side in ((0, right), (1, left)):
            pair_copy(s, p, side).wait_send()
            sum_copy(s, p, side).wait_send()
        return carry

    lax.fori_loop(0, ZS, finish_sides, 0)

    result = jnp.zeros((2 * tok_rows, half), jnp.float32)
    for p in GO_HOME[1]:
        z = (zi - offset(p) + ZS) % ZS
        some = home.at[pl.ds(0, plane - 1 if p == SAME else plane)]
        remote(some, some, home_out.at[p], home_sems.at[p], (right, rank)).wait_recv()
        block = home[at(z, plane)].reshape(plane * 2 * CAP, half)
        result += dot_rows(chosen(z, ones, ones), block)
    result = result.astype(jnp.bfloat16)
    out_tokens[:, pl.ds(0, half)] = result[:tok_rows]
    out_tokens[:, pl.ds(half, half)] = result[tok_rows:]

    def home_sent(p, count):
        some = pl.ds(0, count)
        remote(
            home_send.at[some], home.at[some], home_out.at[p], home_sems.at[p], (right, rank)
        ).wait_send()

    def finish(p, carry):
        @pl.when(p == SAME)
        def _():
            home_sent(p, plane - 1)

        @pl.when(p != SAME)
        def _():
            home_sent(p, plane)

        return carry

    lax.fori_loop(0, ZS, finish, 0)
    for q in range(PARTS):
        for copy in write_copies(q):
            copy.wait()


def write_out(*refs):
    count = (len(refs) - 1) // 2
    sources, targets, sems = refs[:count], refs[count : 2 * count], refs[-1]
    copies = []
    for number, (source, target) in enumerate(zip(sources, targets)):
        step = source.shape[0] // PARTS
        for piece in range(PARTS):
            lines = pl.ds(piece * step, step)
            copies.append(
                pltpu.make_async_copy(source.at[lines], target.at[lines], sems.at[number, piece])
            )
    for copy in copies:
        copy.start()
    for copy in copies:
        copy.wait()


def body(tokens, grad_out, route_weights, expert_ids, gate_weight, up_weight, down_weight):
    tok_rows, width = tokens.shape
    experts = lax.axis_size("expert")
    plane = XS * CORES
    rows = plane * CAP
    total = experts * CAP
    features, hidden = gate_weight.shape[1:]
    half = width // 2
    bf16, f32 = jnp.bfloat16, jnp.float32
    vmem, free = pl.BlockSpec(memory_space=pltpu.VMEM), pl.BlockSpec(memory_space=pl.ANY)
    hbm = pl.BlockSpec(memory_space=pltpu.HBM)
    dma = pltpu.SemaphoreType.DMA
    grads = pl.pallas_call(
        kernel,
        out_shape=(
            jax.ShapeDtypeStruct((tok_rows, width), bf16),
            jax.ShapeDtypeStruct((features, hidden), bf16),
            jax.ShapeDtypeStruct((features, hidden), bf16),
            jax.ShapeDtypeStruct((hidden, features), bf16),
        ),
        in_specs=[vmem, vmem, hbm, hbm, hbm],
        out_specs=(vmem, free, free, free),
        scratch_shapes=[
            pltpu.VMEM((PARTS, 2 * tok_rows, width), bf16),
            pltpu.VMEM((FAR, plane, 2 * CAP, width), bf16),
            pltpu.VMEM((FAR, plane, 2 * CAP, width), bf16),
            pltpu.VMEM((NEAR, plane, PARTS, 2 * CAP, width), bf16),
            pltpu.VMEM((NEAR, plane, PARTS, 2 * CAP, width), bf16),
            pltpu.VMEM((PARTS, total, width), bf16),
            pltpu.VMEM((PARTS, total, width), bf16),
            pltpu.VMEM((features, 2 * hidden), bf16),
            pltpu.VMEM((hidden, features), bf16),
            pltpu.VMEM((total, 2 * hidden), bf16),
            pltpu.VMEM((total, hidden), bf16),
            pltpu.VMEM((hidden, total), bf16),
            pltpu.VMEM((SLOTS, 3, rows, width), f32),
            pltpu.VMEM((2, ZS, rows, half), bf16),
            pltpu.VMEM((2, ZS, rows, half), bf16),
            pltpu.VMEM((2, ZS, rows, width), bf16),
            pltpu.VMEM((2, ZS, rows, width), bf16),
            pltpu.VMEM((experts, 2 * CAP, half), bf16),
            pltpu.VMEM((experts, 2 * CAP, half), bf16),
            dma((3,)),
            dma((6,)),
            dma((6,)),
            dma((FAR,)),
            dma((FAR,)),
            dma((NEAR,)),
            dma((NEAR,)),
            dma((4, FAR)),
            dma((2, FAR)),
            dma((6, FAR)),
            dma((2, ZS)),
            dma((2, ZS)),
            dma((2, ZS)),
            dma((2, ZS)),
            dma((ZS,)),
            dma((ZS,)),
            dma((3, PARTS)),
        ],
        compiler_params=pltpu.CompilerParams(
            collective_id=0, has_side_effects=True, vmem_limit_bytes=47 * 1024 * 1024
        ),
    )(
        jnp.concatenate([expert_ids.T.astype(f32), route_weights.T.astype(f32)], axis=0),
        jnp.concatenate([tokens, grad_out], axis=0),
        gate_weight[0], up_weight[0], down_weight[0],
    )
    grads = pl.pallas_call(
        write_out,
        out_shape=tuple(jax.ShapeDtypeStruct(array.shape, bf16) for array in grads),
        in_specs=[free] * 4,
        out_specs=(free,) * 4,
        scratch_shapes=[dma((4, PARTS))],
        compiler_params=pltpu.CompilerParams(vmem_limit_bytes=2 * 1024 * 1024),
    )(*grads)
    return (grads[0], grads[1][None], grads[2][None], grads[3][None])


def solution(mesh):
    placed = (
        P("expert", "dp"),
        P("expert", "dp"),
        P("expert", None),
        P("expert", None),
        P("expert", None, "dp"),
        P("expert", None, "dp"),
        P("expert", "dp", None),
    )
    return jax.shard_map(
        body,
        mesh=mesh,
        in_specs=placed,
        out_specs=(
            P("expert", "dp"),
            P("expert", None, "dp"),
            P("expert", None, "dp"),
            P("expert", "dp", None),
        ),
        check_vma=False,
    )
```

```python
import jax
import jax.numpy as jnp
from jax import lax
from jax.experimental import pallas as pl
from jax.experimental.pallas import tpu as pltpu
from jax.sharding import PartitionSpec as P

CAP = 8
PARTS = 4
ZS, XS, CORES = 8, 4, 2
MESH = pl.DeviceIdType.MESH

PLANE_OF = (5, 3, 2, 6, 0, 4, 7, 1)
FAR, NEAR, SAME = 5, 3, 4
SLOTS = 6


def code(items):
    return sum(item << (3 * place) for place, item in enumerate(items))


PLANE_CODE = code(PLANE_OF)

GATHER_DONE = ((2,), (4,))
SEND_NEAR = ((2, 4, 6), (0, 1, 2))
ONWARD = ((2, 3, 6, 7, 8), (3, 1, 0, 2, 4))
SPREAD = ((0, 1, 4, 5, 7), (3, 1, 0, 2, 4))
UNPACK = ((7, 11, 12), (0, 2, 1))
COMPUTE = ((7, 8, 10, 15), (0, 1, 2, 3))
REDUCE = ((8, 9, 10, 12, 13, 14, 17, 18), (1, 0, 2, 5, 4, 3, 6, 7))
GO_HOME = ((10, 11, 14, 15, 16, 19, 20, 21), (1, 0, 2, 5, 3, 6, 4, 7))
TURN_WEIGHTS = ((0, 1, 3, 5), (0, 1, 2, 3))
WEIGHTS = ((17, 18), (0, 1))
TURNS = 22


def dot_last(left, right):
    return lax.dot_general(
        left, right, (((1,), (1,)), ((), ())), preferred_element_type=jnp.float32
    )


def turned(block):
    size = block.shape[1]
    diagonal = lax.broadcasted_iota(jnp.int32, (size, size), 0) == (
        lax.broadcasted_iota(jnp.int32, (size, size), 1)
    )
    unit = jnp.where(diagonal, 1.0, 0.0).astype(jnp.bfloat16)
    return dot_last(unit, block).astype(jnp.bfloat16)


def dot_rows(left, right):
    return lax.dot_general(
        left, right, (((0,), (0,)), ((), ())), preferred_element_type=jnp.float32
    )


def kernel(
    table_ref, both_ref, gate_hbm, up_hbm, down_hbm,
    out_tokens, out_gate, out_up, out_down,
    dense, far_send, far_recv, near_send, near_recv, tok, sca, wgu, wdn, wgu_turned, wdn_turned, hid, act, act_turned, part,
    pair_send, pair_recv, sum_send, sum_recv, home_send, home,
    weight_sems, dense_out, dense_sems, far_out, far_sems, near_out, near_sems,
    own_out, onward_out, row_sems, pair_out, pair_sems, sum_out, sum_sems,
    home_out, home_sems, write_sems,
):
    rank = lax.axis_index("expert")
    y = lax.axis_index("dp")
    plane = XS * CORES
    experts = ZS * plane
    rows = plane * CAP
    zi, xi, ci = rank // plane, (rank // CORES) % XS, rank % CORES
    right, left = (y + 1) % PARTS, (y + PARTS - 1) % PARTS
    across = (y + 2) % PARTS
    tok_rows, width = both_ref.shape[0] // 2, both_ref.shape[1]
    half = width // 2
    hidden = act.shape[1]

    def at(row, col):
        return pl.ds(pl.multiple_of(row * col, col), col)

    def offset(p):
        return (PLANE_CODE >> (3 * p)) % 8

    def far_block(j):
        return j + j // 4

    def near_block(n):
        return 4 + n + (n + 1) // 2

    def peer(p, i, sign):
        z = (zi + sign * offset(p) + ZS) % ZS
        x = (xi + sign * (i // CORES) + XS) % XS
        c = (ci + i) % CORES
        return z * plane + x * CORES + c

    def remote(src, dst, out, arrive, device):
        return pltpu.make_async_remote_copy(
            src_ref=src, dst_ref=dst, send_sem=out, recv_sem=arrive,
            device_id=device, device_id_type=MESH,
        )

    barrier = pltpu.get_barrier_semaphore()

    def greet(j, carry):
        pl.semaphore_signal(
            barrier, inc=1, device_id=(y, (rank + j) % experts), device_id_type=MESH
        )
        return carry

    lax.fori_loop(1, experts, greet, 0)
    for side in (left, right):
        pl.semaphore_signal(barrier, inc=1, device_id=(side, rank), device_id_type=MESH)

    weight_copies = [
        pltpu.make_async_copy(gate_hbm, wgu.at[:, pl.ds(0, hidden)], weight_sems.at[0]),
        pltpu.make_async_copy(up_hbm, wgu.at[:, pl.ds(hidden, hidden)], weight_sems.at[1]),
        pltpu.make_async_copy(down_hbm, wdn, weight_sems.at[2]),
    ]
    for copy in weight_copies:
        copy.start()

    def dense_copy(h, q, out, arrive, side):
        some = pl.ds(h * tok_rows, tok_rows)
        return remote(
            both_ref.at[some] if q is y else dense.at[q, some], dense.at[q, some],
            out, dense_sems.at[arrive], (side, rank),
        )

    def dense_own():
        return [
            dense_copy(0, y, dense_out.at[0], 0, right),
            dense_copy(1, y, dense_out.at[1], 3, left),
            dense_copy(1, y, dense_out.at[2], 1, right),
            dense_copy(0, y, dense_out.at[3], 2, left),
        ]

    def dense_onward():
        return [
            dense_copy(0, left, dense_out.at[4], 4, right),
            dense_copy(1, right, dense_out.at[5], 5, left),
        ]

    def dense_arrival(h, q, arrive):
        dense_copy(h, q, dense_out.at[0], arrive, right).wait_recv()

    pl.semaphore_wait(barrier, experts + 1)
    for copy in dense_own():
        copy.start()
    dense[y] = both_ref[...]

    ids = jnp.floor(table_ref[...] * 0.5)
    weights = table_ref[...] - 2.0 * ids
    numbers = lax.broadcasted_iota(jnp.int32, (experts, tok_rows), 0).astype(jnp.float32)
    hits = [numbers == ids[c : c + 1] for c in range(2)]
    before = lax.broadcasted_iota(jnp.int32, (tok_rows, tok_rows), 0) < (
        lax.broadcasted_iota(jnp.int32, (tok_rows, tok_rows), 1)
    )
    earlier = jnp.dot(
        jnp.where(hits[0] | hits[1], 1.0, 0.0).astype(jnp.bfloat16),
        jnp.where(before, 1.0, 0.0).astype(jnp.bfloat16),
        preferred_element_type=jnp.float32,
    )
    place = [
        jnp.sum(jnp.where(hits[c], earlier, 0.0), axis=0, keepdims=True)
        + ids[c : c + 1] * (2 * CAP)
        for c in range(2)
    ]

    def chosen(z, first, second):
        line = lax.broadcasted_iota(jnp.int32, (plane * 2 * CAP, tok_rows), 0)
        line = (line + z * (plane * 2 * CAP)).astype(jnp.float32)
        halves = [
            jnp.where(line == place[0] + shift, value[0:1], 0.0)
            + jnp.where(line == place[1] + shift, value[1:2], 0.0)
            for shift, value in ((0.0, first), (float(CAP), second))
        ]
        return jnp.concatenate(halves, axis=1).astype(jnp.bfloat16)

    ones = jnp.ones_like(weights)

    def picks(p):
        return chosen((zi - offset(p) + ZS) % ZS, ones, weights)

    def pick(which, q):
        picked = jnp.dot(which, dense[q], preferred_element_type=jnp.float32)
        return picked.astype(jnp.bfloat16).reshape(plane, 2 * CAP, width)

    def far_copy(j, i):
        target = peer(far_block(j), i, -1)
        return remote(
            far_send.at[j, target % plane], far_recv.at[j, i],
            far_out.at[j], far_sems.at[j], (y, target),
        )

    def far_whole(j):
        return remote(far_send.at[j], far_recv.at[j], far_out.at[j], far_sems.at[j], (right, rank))

    def pack_far(j):
        far_send[j] = pick(picks(far_block(j)), y)

    def dispatch_far(j, carry):
        def one(i, inner):
            far_copy(j, i).start()
            return inner

        return lax.fori_loop(0, plane, one, carry)

    def near_copy(n, i):
        target = peer(near_block(n), i, -1)
        return remote(
            near_send.at[n, target % plane], near_recv.at[n, i],
            near_out.at[n], near_sems.at[n], (y, target),
        )

    def near_whole(n, first):
        some = pl.ds(first, plane - first)
        return remote(
            near_send.at[n, some], near_recv.at[n, some],
            near_out.at[n], near_sems.at[n], (right, rank),
        )

    def dispatch_near(n):
        which = picks(near_block(n))
        for q in range(PARTS):
            near_send[n, :, q] = pick(which, q)

        def one(i, inner):
            near_copy(n, i).start()
            return inner

        same = near_block(n) == SAME

        @pl.when(same)
        def _():
            near_recv[n, 0] = near_send[n, rank % plane]
            lax.fori_loop(1, plane, one, 0)

        @pl.when(jnp.logical_not(same))
        def _():
            lax.fori_loop(0, plane, one, 0)

    def side_copy(buf, q, p, out, arrive, side):
        block = buf.at[q, at(p, rows)]
        return remote(block, block, out, arrive, (side, rank))

    def own_copies(j):
        p = far_block(j)
        return [
            side_copy(tok, y, p, own_out.at[0, j], row_sems.at[0, j], right),
            side_copy(sca, y, p, own_out.at[1, j], row_sems.at[3, j], left),
            side_copy(sca, y, p, own_out.at[2, j], row_sems.at[1, j], right),
            side_copy(tok, y, p, own_out.at[3, j], row_sems.at[2, j], left),
        ]

    def onward_copies(j):
        p = far_block(j)
        return [
            side_copy(tok, left, p, onward_out.at[0, j], row_sems.at[4, j], right),
            side_copy(sca, right, p, onward_out.at[1, j], row_sems.at[5, j], left),
        ]

    def arrival(buf, q, j, arrive):
        side_copy(
            buf, q, far_block(j), own_out.at[0, j], row_sems.at[arrive, j], right
        ).wait_recv()

    def separate(got, q, p):
        got = got.astype(jnp.float32)
        mine = at(p, rows)
        tok[q, mine, :] = got[:, :CAP, :].reshape(rows, width).astype(jnp.bfloat16)
        sca[q, mine, :] = got[:, CAP:, :].reshape(rows, width).astype(jnp.bfloat16)

    def spread(j):
        far_whole(j).wait_recv()
        separate(far_recv[j], y, far_block(j))
        for copy in own_copies(j):
            copy.start()

    def onward(j):
        copies = onward_copies(j)
        arrival(tok, left, j, 0)
        copies[0].start()
        arrival(sca, right, j, 3)
        copies[1].start()

    def unpack(n):
        p = near_block(n)

        @pl.when(p == SAME)
        def _():
            near_whole(n, 1).wait_recv()

        @pl.when(p != SAME)
        def _():
            near_whole(n, 0).wait_recv()

        for q in range(PARTS):
            separate(near_recv[n, :, q], q, p)

    def pair_copy(s, p, side):
        return remote(
            pair_send.at[s, p], pair_recv.at[s, p], pair_out.at[s, p], pair_sems.at[s, p],
            (side, rank),
        )

    def sum_copy(s, p, side):
        return remote(
            sum_send.at[s, p], sum_recv.at[s, p], sum_out.at[s, p], sum_sems.at[s, p],
            (side, rank),
        )

    def turn_weights(q):
        tile = min(256, width)

        def one(j, carry):
            lines = pl.ds(pl.multiple_of(q * width + j * tile, tile), tile)
            for h in range(2):
                some = pl.ds(h * hidden, hidden)
                wgu_turned[some, lines] = turned(wgu[lines, some])
            wdn_turned[lines, :] = turned(wdn[:, lines])
            return carry

        lax.fori_loop(0, width // tile, one, 0)

    def compute(pair):
        mine = at(pair, 2 * rows)

        def gathered(j):
            arrival(sca, left, j, 1)
            arrival(tok, right, j, 2)
            arrival(tok, across, j, 4)
            arrival(sca, across, j, 5)

        @pl.when(pair < 2)
        def _():
            gathered(2 * pair)
            gathered(2 * pair + 1)

        @pl.when(pair == 2)
        def _():
            gathered(4)

        pre = jnp.zeros((2 * rows, 2 * hidden), jnp.float32)
        grad_act = jnp.zeros((2 * rows, hidden), jnp.float32)
        for q in range(PARTS):
            pre += jnp.dot(
                tok[q, mine, :], wgu[pl.ds(q * width, width), :],
                preferred_element_type=jnp.float32,
            )
            grad_act += jnp.dot(
                sca[q, mine, :], wdn_turned[pl.ds(q * width, width), :],
                preferred_element_type=jnp.float32,
            )
        gate_pre, up_pre = pre[:, :hidden], pre[:, hidden:]
        sigmoid_gate = 1.0 / (1.0 + jnp.exp(-gate_pre))
        swish_gate = gate_pre * sigmoid_gate
        act[mine, :] = (swish_gate * up_pre).astype(jnp.bfloat16)
        hid[mine, :] = jnp.concatenate(
            [
                grad_act * up_pre * sigmoid_gate * (1.0 + gate_pre * (1.0 - sigmoid_gate)),
                grad_act * swish_gate,
            ],
            axis=1,
        ).astype(jnp.bfloat16)

        def back(q):
            return jnp.dot(
                hid[mine, :], wgu_turned[:, at(q, width)], preferred_element_type=jnp.float32
            )

        far = back(across).astype(jnp.bfloat16)
        for i in range(2):
            p = 2 * pair + i
            pair_send[0, p] = far[i * rows : (i + 1) * rows, :half]
            pair_send[1, p] = far[i * rows : (i + 1) * rows, half:]
            pair_copy(0, p, right).start()
            pair_copy(1, p, left).start()
        for kept, q in enumerate((right, left, y)):
            mine_part = back(q)
            for i in range(2):
                part[(2 * pair + i) % SLOTS, kept] = mine_part[i * rows : (i + 1) * rows]

    def reduce_sides(p):
        slot = p % SLOTS
        pair_copy(0, p, right).wait_recv()
        near = part[slot, 0]
        sum_send[0, p] = jnp.concatenate(
            [near[:, :half] + pair_recv[0, p].astype(jnp.float32), near[:, half:]], axis=1
        ).astype(jnp.bfloat16)
        sum_copy(0, p, right).start()
        pair_copy(1, p, left).wait_recv()
        near = part[slot, 1]
        sum_send[1, p] = jnp.concatenate(
            [near[:, :half], near[:, half:] + pair_recv[1, p].astype(jnp.float32)], axis=1
        ).astype(jnp.bfloat16)
        sum_copy(1, p, left).start()

    def home_copy(p, i):
        return remote(
            home_send.at[p * plane + i], home.at[rank], home_out.at[p], home_sems.at[p],
            (y, peer(p, i, 1)),
        )

    def go_home(p):
        sum_copy(0, p, right).wait_recv()
        sum_copy(1, p, left).wait_recv()
        total = (
            part[p % SLOTS, 2]
            + sum_recv[0, p].astype(jnp.float32)
            + sum_recv[1, p].astype(jnp.float32)
        ).reshape(plane, CAP, width)
        home_send[at(p, plane)] = jnp.concatenate(
            [total[:, :, :half], total[:, :, half:]], axis=1
        ).astype(jnp.bfloat16)

        def one(i, carry):
            home_copy(p, i).start()
            return carry

        @pl.when(p == SAME)
        def _():
            home[rank] = home_send[SAME * plane]
            lax.fori_loop(1, plane, one, 0)

        @pl.when(p != SAME)
        def _():
            lax.fori_loop(0, plane, one, 0)

    def write_copies(q):
        lines = at(q, width)
        return [
            pltpu.make_async_copy(
                wgu.at[lines, pl.ds(0, hidden)], out_gate.at[lines], write_sems.at[0, q]
            ),
            pltpu.make_async_copy(
                wgu.at[lines, pl.ds(hidden, hidden)], out_up.at[lines], write_sems.at[1, q]
            ),
            pltpu.make_async_copy(wdn.at[:, lines], out_down.at[:, lines], write_sems.at[2, q]),
        ]

    def weight_grads(q):
        tile = min(256, width)

        @pl.when(q == 0)
        def _():
            act_turned[...] = turned(act[...])

        def one(j, carry):
            cols = at(j, tile)
            lines = pl.ds(pl.multiple_of(q * width + j * tile, tile), tile)
            wgu[lines, :] = jnp.dot(
                turned(tok[q, :, cols]), hid[...], preferred_element_type=jnp.float32
            ).astype(jnp.bfloat16)
            wdn[:, lines] = jnp.dot(
                act_turned[...], sca[q, :, cols], preferred_element_type=jnp.float32
            ).astype(jnp.bfloat16)
            return carry

        lax.fori_loop(0, width // tile, one, 0)
        for copy in write_copies(q):
            copy.start()

    def next_far(j, carry):
        pack_far(j)
        return dispatch_far(j, carry)

    lax.fori_loop(1, 4, next_far, 0)
    copies = dense_onward()
    dense_arrival(0, left, 0)
    copies[0].start()
    dense_arrival(1, right, 3)
    copies[1].start()
    next_far(0, 0)
    for copy in weight_copies:
        copy.wait()

    def gather_done(j):
        dense_arrival(1, left, 1)
        dense_arrival(0, right, 2)
        dense_arrival(0, across, 4)
        dense_arrival(1, across, 5)
        next_far(j, 0)

    def turn(t, carry):
        def stage(plan, work):
            turns, blocks = plan
            now = t == turns[0]
            for at_turn in turns[1:]:
                now = now | (t == at_turn)

            @pl.when(now)
            def _():
                index = 0
                for at_turn in turns:
                    index = index + jnp.where(t > at_turn, 1, 0)
                work((code(blocks) >> (3 * index)) % 8)

        stage(GATHER_DONE, gather_done)
        stage(SEND_NEAR, dispatch_near)
        stage(ONWARD, onward)
        stage(SPREAD, spread)
        stage(UNPACK, unpack)
        stage(COMPUTE, compute)
        stage(REDUCE, reduce_sides)
        stage(GO_HOME, go_home)
        stage(TURN_WEIGHTS, turn_weights)
        stage(WEIGHTS, weight_grads)
        return carry

    lax.fori_loop(0, TURNS, turn, 0)
    for q in range(len(WEIGHTS[0]), PARTS):
        weight_grads(q)

    for copy in dense_own() + dense_onward():
        copy.wait_send()

    def finish_far(j, carry):
        far_whole(j).wait_send()
        for copy in own_copies(j) + onward_copies(j):
            copy.wait_send()
        return carry

    lax.fori_loop(0, FAR, finish_far, 0)
    for n in range(NEAR):
        near_whole(n, 1 if near_block(n) == SAME else 0).wait_send()

    def finish_sides(p, carry):
        for s, side in ((0, right), (1, left)):
            pair_copy(s, p, side).wait_send()
            sum_copy(s, p, side).wait_send()
        return carry

    lax.fori_loop(0, ZS, finish_sides, 0)

    result = jnp.zeros((2 * tok_rows, half), jnp.float32)
    for p in GO_HOME[1]:
        z = (zi - offset(p) + ZS) % ZS
        some = home.at[pl.ds(0, plane - 1 if p == SAME else plane)]
        remote(some, some, home_out.at[p], home_sems.at[p], (right, rank)).wait_recv()
        block = home[at(z, plane)].reshape(plane * 2 * CAP, half)
        result += dot_rows(chosen(z, ones, ones), block)
    result = result.astype(jnp.bfloat16)
    out_tokens[:, pl.ds(0, half)] = result[:tok_rows]
    out_tokens[:, pl.ds(half, half)] = result[tok_rows:]

    def home_sent(p, count):
        some = pl.ds(0, count)
        remote(
            home_send.at[some], home.at[some], home_out.at[p], home_sems.at[p], (right, rank)
        ).wait_send()

    def finish(p, carry):
        @pl.when(p == SAME)
        def _():
            home_sent(p, plane - 1)

        @pl.when(p != SAME)
        def _():
            home_sent(p, plane)

        return carry

    lax.fori_loop(0, ZS, finish, 0)
    for q in range(PARTS):
        for copy in write_copies(q):
            copy.wait()


def write_out(*refs):
    count = (len(refs) - 1) // 2
    sources, targets, sems = refs[:count], refs[count : 2 * count], refs[-1]
    copies = []
    for number, (source, target) in enumerate(zip(sources, targets)):
        step = source.shape[0] // PARTS
        for piece in range(PARTS):
            lines = pl.ds(piece * step, step)
            copies.append(
                pltpu.make_async_copy(source.at[lines], target.at[lines], sems.at[number, piece])
            )
    for copy in copies:
        copy.start()
    for copy in copies:
        copy.wait()


def body(tokens, grad_out, route_weights, expert_ids, gate_weight, up_weight, down_weight):
    tok_rows, width = tokens.shape
    experts = lax.axis_size("expert")
    plane = XS * CORES
    rows = plane * CAP
    total = experts * CAP
    features, hidden = gate_weight.shape[1:]
    half = width // 2
    bf16, f32 = jnp.bfloat16, jnp.float32
    vmem, free = pl.BlockSpec(memory_space=pltpu.VMEM), pl.BlockSpec(memory_space=pl.ANY)
    hbm = pl.BlockSpec(memory_space=pltpu.HBM)
    dma = pltpu.SemaphoreType.DMA
    grads = pl.pallas_call(
        kernel,
        out_shape=(
            jax.ShapeDtypeStruct((tok_rows, width), bf16),
            jax.ShapeDtypeStruct((features, hidden), bf16),
            jax.ShapeDtypeStruct((features, hidden), bf16),
            jax.ShapeDtypeStruct((hidden, features), bf16),
        ),
        in_specs=[vmem, vmem, hbm, hbm, hbm],
        out_specs=(vmem, free, free, free),
        scratch_shapes=[
            pltpu.VMEM((PARTS, 2 * tok_rows, width), bf16),
            pltpu.VMEM((FAR, plane, 2 * CAP, width), bf16),
            pltpu.VMEM((FAR, plane, 2 * CAP, width), bf16),
            pltpu.VMEM((NEAR, plane, PARTS, 2 * CAP, width), bf16),
            pltpu.VMEM((NEAR, plane, PARTS, 2 * CAP, width), bf16),
            pltpu.VMEM((PARTS, total, width), bf16),
            pltpu.VMEM((PARTS, total, width), bf16),
            pltpu.VMEM((features, 2 * hidden), bf16),
            pltpu.VMEM((hidden, features), bf16),
            pltpu.VMEM((2 * hidden, features), bf16),
            pltpu.VMEM((features, hidden), bf16),
            pltpu.VMEM((total, 2 * hidden), bf16),
            pltpu.VMEM((total, hidden), bf16),
            pltpu.VMEM((hidden, total), bf16),
            pltpu.VMEM((SLOTS, 3, rows, width), f32),
            pltpu.VMEM((2, ZS, rows, half), bf16),
            pltpu.VMEM((2, ZS, rows, half), bf16),
            pltpu.VMEM((2, ZS, rows, width), bf16),
            pltpu.VMEM((2, ZS, rows, width), bf16),
            pltpu.VMEM((experts, 2 * CAP, half), bf16),
            pltpu.VMEM((experts, 2 * CAP, half), bf16),
            dma((3,)),
            dma((6,)),
            dma((6,)),
            dma((FAR,)),
            dma((FAR,)),
            dma((NEAR,)),
            dma((NEAR,)),
            dma((4, FAR)),
            dma((2, FAR)),
            dma((6, FAR)),
            dma((2, ZS)),
            dma((2, ZS)),
            dma((2, ZS)),
            dma((2, ZS)),
            dma((ZS,)),
            dma((ZS,)),
            dma((3, PARTS)),
        ],
        compiler_params=pltpu.CompilerParams(
            collective_id=0, has_side_effects=True, vmem_limit_bytes=47 * 1024 * 1024
        ),
    )(
        (2.0 * expert_ids.astype(f32) + route_weights.astype(f32)).T,
        jnp.concatenate([tokens, grad_out], axis=0),
        gate_weight[0], up_weight[0], down_weight[0],
    )
    grads = pl.pallas_call(
        write_out,
        out_shape=tuple(jax.ShapeDtypeStruct(array.shape, bf16) for array in grads),
        in_specs=[free] * 4,
        out_specs=(free,) * 4,
        scratch_shapes=[dma((4, PARTS))],
        compiler_params=pltpu.CompilerParams(vmem_limit_bytes=2 * 1024 * 1024),
    )(*grads)
    return (grads[0], grads[1][None], grads[2][None], grads[3][None])


def solution(mesh):
    placed = (
        P("expert", "dp"),
        P("expert", "dp"),
        P("expert", None),
        P("expert", None),
        P("expert", None, "dp"),
        P("expert", None, "dp"),
        P("expert", "dp", None),
    )
    return jax.shard_map(
        body,
        mesh=mesh,
        in_specs=placed,
        out_specs=(
            P("expert", "dp"),
            P("expert", None, "dp"),
            P("expert", None, "dp"),
            P("expert", "dp", None),
        ),
        check_vma=False,
    )
```

```python
import jax
import jax.numpy as jnp
from jax import lax
from jax.experimental import pallas as pl
from jax.experimental.pallas import tpu as pltpu
from jax.sharding import PartitionSpec as P

CAP = 8
PARTS = 4
ZS, XS, CORES = 8, 4, 2
MESH = pl.DeviceIdType.MESH

PLANE_OF = (5, 3, 2, 6, 0, 4, 7, 1)
FAR, NEAR, SAME = 5, 3, 4
SLOTS = 6


def code(items):
    return sum(item << (3 * place) for place, item in enumerate(items))


PLANE_CODE = code(PLANE_OF)

GATHER_DONE = ((2,), (4,))
SEND_NEAR = ((2, 3, 4, 5, 6, 7), (0, 1, 2, 3, 4, 5))
ONWARD = ((2, 3, 6, 7, 8), (3, 1, 0, 2, 4))
SPREAD = ((0, 1, 4, 5, 7), (3, 1, 0, 2, 4))
UNPACK = ((7, 15, 16), (0, 2, 1))
COMPUTE = ((7, 8, 10, 16), (0, 1, 2, 3))
REDUCE = ((8, 9, 10, 12, 13, 14, 18, 19), (1, 0, 2, 5, 4, 3, 6, 7))
GO_HOME = ((10, 11, 14, 16, 17, 20, 21, 22), (1, 0, 2, 5, 3, 6, 4, 7))
TURN_WEIGHTS = ((0, 1, 3, 5), (0, 1, 2, 3))
WEIGHTS = ((18, 19), (0, 1))
TURNS = 23


def dot_last(left, right):
    return lax.dot_general(
        left, right, (((1,), (1,)), ((), ())), preferred_element_type=jnp.float32
    )


def turned(block):
    size = block.shape[1]
    diagonal = lax.broadcasted_iota(jnp.int32, (size, size), 0) == (
        lax.broadcasted_iota(jnp.int32, (size, size), 1)
    )
    unit = jnp.where(diagonal, 1.0, 0.0).astype(jnp.bfloat16)
    return dot_last(unit, block).astype(jnp.bfloat16)


def dot_rows(left, right):
    return lax.dot_general(
        left, right, (((0,), (0,)), ((), ())), preferred_element_type=jnp.float32
    )


def kernel(
    table_ref, both_ref, gate_hbm, up_hbm, down_hbm,
    out_tokens, out_gate, out_up, out_down,
    dense, far_send, far_recv, near_send, near_recv, tok, sca, wgu, wdn, wgu_turned, wdn_turned, hid, act, act_turned, part,
    pair_send, pair_recv, sum_send, sum_recv, home_send, home,
    weight_sems, dense_out, dense_sems, far_out, far_sems, near_out, near_sems,
    own_out, onward_out, row_sems, pair_out, pair_sems, sum_out, sum_sems,
    home_out, home_sems, write_sems,
):
    rank = lax.axis_index("expert")
    y = lax.axis_index("dp")
    plane = XS * CORES
    experts = ZS * plane
    rows = plane * CAP
    zi, xi, ci = rank // plane, (rank // CORES) % XS, rank % CORES
    right, left = (y + 1) % PARTS, (y + PARTS - 1) % PARTS
    across = (y + 2) % PARTS
    tok_rows, width = both_ref.shape[0] // 2, both_ref.shape[1]
    half = width // 2
    hidden = act.shape[1]

    def at(row, col):
        return pl.ds(pl.multiple_of(row * col, col), col)

    def offset(p):
        return (PLANE_CODE >> (3 * p)) % 8

    def far_block(j):
        return j + j // 4

    def near_block(n):
        return 4 + n + (n + 1) // 2

    def peer(p, i, sign):
        z = (zi + sign * offset(p) + ZS) % ZS
        x = (xi + sign * (i // CORES) + XS) % XS
        c = (ci + i) % CORES
        return z * plane + x * CORES + c

    def remote(src, dst, out, arrive, device):
        return pltpu.make_async_remote_copy(
            src_ref=src, dst_ref=dst, send_sem=out, recv_sem=arrive,
            device_id=device, device_id_type=MESH,
        )

    barrier = pltpu.get_barrier_semaphore()

    def greet(j, carry):
        pl.semaphore_signal(
            barrier, inc=1, device_id=(y, (rank + j) % experts), device_id_type=MESH
        )
        return carry

    for side in (left, right):
        pl.semaphore_signal(barrier, inc=1, device_id=(side, rank), device_id_type=MESH)
    lax.fori_loop(1, experts, greet, 0)

    weight_copies = [
        pltpu.make_async_copy(gate_hbm, wgu.at[:, pl.ds(0, hidden)], weight_sems.at[0]),
        pltpu.make_async_copy(up_hbm, wgu.at[:, pl.ds(hidden, hidden)], weight_sems.at[1]),
        pltpu.make_async_copy(down_hbm, wdn, weight_sems.at[2]),
    ]
    for copy in weight_copies:
        copy.start()

    def dense_copy(h, q, out, arrive, side):
        some = pl.ds(h * tok_rows, tok_rows)
        return remote(
            both_ref.at[some] if q is y else dense.at[q, some], dense.at[q, some],
            out, dense_sems.at[arrive], (side, rank),
        )

    def dense_own():
        return [
            dense_copy(0, y, dense_out.at[0], 0, right),
            dense_copy(1, y, dense_out.at[1], 3, left),
            dense_copy(1, y, dense_out.at[2], 1, right),
            dense_copy(0, y, dense_out.at[3], 2, left),
        ]

    def dense_onward():
        return [
            dense_copy(0, left, dense_out.at[4], 4, right),
            dense_copy(1, right, dense_out.at[5], 5, left),
        ]

    def dense_arrival(h, q, arrive):
        dense_copy(h, q, dense_out.at[0], arrive, right).wait_recv()

    pl.semaphore_wait(barrier, experts + 1)
    for copy in dense_own():
        copy.start()
    dense[y] = both_ref[...]

    ids = jnp.floor(table_ref[...] * 0.5)
    weights = table_ref[...] - 2.0 * ids
    numbers = lax.broadcasted_iota(jnp.int32, (experts, tok_rows), 0).astype(jnp.float32)
    hits = [numbers == ids[c : c + 1] for c in range(2)]
    before = lax.broadcasted_iota(jnp.int32, (tok_rows, tok_rows), 0) < (
        lax.broadcasted_iota(jnp.int32, (tok_rows, tok_rows), 1)
    )
    earlier = jnp.dot(
        jnp.where(hits[0] | hits[1], 1.0, 0.0).astype(jnp.bfloat16),
        jnp.where(before, 1.0, 0.0).astype(jnp.bfloat16),
        preferred_element_type=jnp.float32,
    )
    place = [
        jnp.sum(jnp.where(hits[c], earlier, 0.0), axis=0, keepdims=True)
        + ids[c : c + 1] * (2 * CAP)
        for c in range(2)
    ]

    def chosen(z, first, second):
        line = lax.broadcasted_iota(jnp.int32, (plane * 2 * CAP, tok_rows), 0)
        line = (line + z * (plane * 2 * CAP)).astype(jnp.float32)
        halves = [
            jnp.where(line == place[0] + shift, value[0:1], 0.0)
            + jnp.where(line == place[1] + shift, value[1:2], 0.0)
            for shift, value in ((0.0, first), (float(CAP), second))
        ]
        return jnp.concatenate(halves, axis=1).astype(jnp.bfloat16)

    ones = jnp.ones_like(weights)

    def picks(p):
        return chosen((zi - offset(p) + ZS) % ZS, ones, weights)

    def pick(which, q):
        picked = jnp.dot(which, dense[q], preferred_element_type=jnp.float32)
        return picked.astype(jnp.bfloat16).reshape(plane, 2 * CAP, width)

    def far_copy(j, i):
        target = peer(far_block(j), i, -1)
        return remote(
            far_send.at[j, target % plane], far_recv.at[j, i],
            far_out.at[j], far_sems.at[j], (y, target),
        )

    def far_whole(j):
        return remote(far_send.at[j], far_recv.at[j], far_out.at[j], far_sems.at[j], (right, rank))

    def pack_far(j):
        far_send[j] = pick(picks(far_block(j)), y)

    def dispatch_far(j, carry):
        def one(i, inner):
            far_copy(j, i).start()
            return inner

        return lax.fori_loop(0, plane, one, carry)

    def near_copy(n, i):
        target = peer(near_block(n), i, -1)
        return remote(
            near_send.at[n, target % plane], near_recv.at[n, i],
            near_out.at[n], near_sems.at[n], (y, target),
        )

    def near_whole(n, first):
        some = pl.ds(first, plane - first)
        return remote(
            near_send.at[n, some], near_recv.at[n, some],
            near_out.at[n], near_sems.at[n], (right, rank),
        )

    def dispatch_near(m):
        n, second = m // 2, m % 2

        @pl.when(second == 0)
        def _():
            which = picks(near_block(n))
            for q in range(PARTS):
                near_send[n, :, q] = pick(which, q)

        def one(i, inner):
            near_copy(n, i).start()
            return inner

        @pl.when(m == 0)
        def _():
            near_recv[0, 0] = near_send[0, rank % plane]

        first = second * (plane // 2)
        lax.fori_loop(jnp.where(m == 0, 1, first), first + plane // 2, one, 0)

    def side_copy(buf, q, p, out, arrive, side):
        block = buf.at[q, at(p, rows)]
        return remote(block, block, out, arrive, (side, rank))

    def own_copies(j):
        p = far_block(j)
        return [
            side_copy(tok, y, p, own_out.at[0, j], row_sems.at[0, j], right),
            side_copy(sca, y, p, own_out.at[1, j], row_sems.at[3, j], left),
            side_copy(sca, y, p, own_out.at[2, j], row_sems.at[1, j], right),
            side_copy(tok, y, p, own_out.at[3, j], row_sems.at[2, j], left),
        ]

    def onward_copies(j):
        p = far_block(j)
        return [
            side_copy(tok, left, p, onward_out.at[0, j], row_sems.at[4, j], right),
            side_copy(sca, right, p, onward_out.at[1, j], row_sems.at[5, j], left),
        ]

    def arrival(buf, q, j, arrive):
        side_copy(
            buf, q, far_block(j), own_out.at[0, j], row_sems.at[arrive, j], right
        ).wait_recv()

    def separate(got, q, p):
        got = got.astype(jnp.float32)
        mine = at(p, rows)
        tok[q, mine, :] = got[:, :CAP, :].reshape(rows, width).astype(jnp.bfloat16)
        sca[q, mine, :] = got[:, CAP:, :].reshape(rows, width).astype(jnp.bfloat16)

    def spread(j):
        far_whole(j).wait_recv()
        separate(far_recv[j], y, far_block(j))
        for copy in own_copies(j):
            copy.start()

    def onward(j):
        copies = onward_copies(j)
        arrival(tok, left, j, 0)
        copies[0].start()
        arrival(sca, right, j, 3)
        copies[1].start()

    def unpack(n):
        p = near_block(n)

        @pl.when(p == SAME)
        def _():
            near_whole(n, 1).wait_recv()

        @pl.when(p != SAME)
        def _():
            near_whole(n, 0).wait_recv()

        for q in range(PARTS):
            separate(near_recv[n, :, q], q, p)

    def pair_copy(s, p, side):
        return remote(
            pair_send.at[s, p], pair_recv.at[s, p], pair_out.at[s, p], pair_sems.at[s, p],
            (side, rank),
        )

    def sum_copy(s, p, side):
        return remote(
            sum_send.at[s, p], sum_recv.at[s, p], sum_out.at[s, p], sum_sems.at[s, p],
            (side, rank),
        )

    def turn_weights(q):
        tile = min(256, width)

        def one(j, carry):
            lines = pl.ds(pl.multiple_of(q * width + j * tile, tile), tile)
            for h in range(2):
                some = pl.ds(h * hidden, hidden)
                wgu_turned[some, lines] = turned(wgu[lines, some])
            wdn_turned[lines, :] = turned(wdn[:, lines])
            return carry

        lax.fori_loop(0, width // tile, one, 0)

    def compute(pair):
        mine = at(pair, 2 * rows)

        def gathered(j):
            arrival(sca, left, j, 1)
            arrival(tok, right, j, 2)
            arrival(tok, across, j, 4)
            arrival(sca, across, j, 5)

        @pl.when(pair < 2)
        def _():
            gathered(2 * pair)
            gathered(2 * pair + 1)

        @pl.when(pair == 2)
        def _():
            gathered(4)

        pre = jnp.zeros((2 * rows, 2 * hidden), jnp.float32)
        grad_act = jnp.zeros((2 * rows, hidden), jnp.float32)
        for q in range(PARTS):
            pre += jnp.dot(
                tok[q, mine, :], wgu[pl.ds(q * width, width), :],
                preferred_element_type=jnp.float32,
            )
            grad_act += jnp.dot(
                sca[q, mine, :], wdn_turned[pl.ds(q * width, width), :],
                preferred_element_type=jnp.float32,
            )
        gate_pre, up_pre = pre[:, :hidden], pre[:, hidden:]
        sigmoid_gate = 1.0 / (1.0 + jnp.exp(-gate_pre))
        swish_gate = gate_pre * sigmoid_gate
        act[mine, :] = (swish_gate * up_pre).astype(jnp.bfloat16)
        hid[mine, :] = jnp.concatenate(
            [
                grad_act * up_pre * sigmoid_gate * (1.0 + gate_pre * (1.0 - sigmoid_gate)),
                grad_act * swish_gate,
            ],
            axis=1,
        ).astype(jnp.bfloat16)

        def back(q):
            return jnp.dot(
                hid[mine, :], wgu_turned[:, at(q, width)], preferred_element_type=jnp.float32
            )

        far = back(across).astype(jnp.bfloat16)
        for i in range(2):
            p = 2 * pair + i
            pair_send[0, p] = far[i * rows : (i + 1) * rows, :half]
            pair_send[1, p] = far[i * rows : (i + 1) * rows, half:]
            pair_copy(0, p, right).start()
            pair_copy(1, p, left).start()
        for kept, q in enumerate((right, left, y)):
            mine_part = back(q)
            for i in range(2):
                part[(2 * pair + i) % SLOTS, kept] = mine_part[i * rows : (i + 1) * rows]

    def reduce_sides(p):
        slot = p % SLOTS
        pair_copy(0, p, right).wait_recv()
        near = part[slot, 0]
        sum_send[0, p] = jnp.concatenate(
            [near[:, :half] + pair_recv[0, p].astype(jnp.float32), near[:, half:]], axis=1
        ).astype(jnp.bfloat16)
        sum_copy(0, p, right).start()
        pair_copy(1, p, left).wait_recv()
        near = part[slot, 1]
        sum_send[1, p] = jnp.concatenate(
            [near[:, :half], near[:, half:] + pair_recv[1, p].astype(jnp.float32)], axis=1
        ).astype(jnp.bfloat16)
        sum_copy(1, p, left).start()

    def home_copy(p, i):
        return remote(
            home_send.at[p * plane + i], home.at[rank], home_out.at[p], home_sems.at[p],
            (y, peer(p, i, 1)),
        )

    def go_home(p):
        sum_copy(0, p, right).wait_recv()
        sum_copy(1, p, left).wait_recv()
        total = (
            part[p % SLOTS, 2]
            + sum_recv[0, p].astype(jnp.float32)
            + sum_recv[1, p].astype(jnp.float32)
        ).reshape(plane, CAP, width)
        home_send[at(p, plane)] = jnp.concatenate(
            [total[:, :, :half], total[:, :, half:]], axis=1
        ).astype(jnp.bfloat16)

        def one(i, carry):
            home_copy(p, i).start()
            return carry

        @pl.when(p == SAME)
        def _():
            home[rank] = home_send[SAME * plane]
            lax.fori_loop(1, plane, one, 0)

        @pl.when(p != SAME)
        def _():
            lax.fori_loop(0, plane, one, 0)

    def write_copies(q):
        lines = at(q, width)
        return [
            pltpu.make_async_copy(
                wgu.at[lines, pl.ds(0, hidden)], out_gate.at[lines], write_sems.at[0, q]
            ),
            pltpu.make_async_copy(
                wgu.at[lines, pl.ds(hidden, hidden)], out_up.at[lines], write_sems.at[1, q]
            ),
            pltpu.make_async_copy(wdn.at[:, lines], out_down.at[:, lines], write_sems.at[2, q]),
        ]

    def weight_grads(q):
        tile = min(256, width)

        @pl.when(q == 0)
        def _():
            act_turned[...] = turned(act[...])

        def one(j, carry):
            cols = at(j, tile)
            lines = pl.ds(pl.multiple_of(q * width + j * tile, tile), tile)
            wgu[lines, :] = jnp.dot(
                turned(tok[q, :, cols]), hid[...], preferred_element_type=jnp.float32
            ).astype(jnp.bfloat16)
            wdn[:, lines] = jnp.dot(
                act_turned[...], sca[q, :, cols], preferred_element_type=jnp.float32
            ).astype(jnp.bfloat16)
            return carry

        lax.fori_loop(0, width // tile, one, 0)
        for copy in write_copies(q):
            copy.start()

    def next_far(j, carry):
        pack_far(j)
        return dispatch_far(j, carry)

    lax.fori_loop(1, 4, next_far, 0)
    copies = dense_onward()
    dense_arrival(0, left, 0)
    copies[0].start()
    dense_arrival(1, right, 3)
    copies[1].start()
    next_far(0, 0)
    for copy in weight_copies:
        copy.wait()

    def gather_done(j):
        dense_arrival(1, left, 1)
        dense_arrival(0, right, 2)
        dense_arrival(0, across, 4)
        dense_arrival(1, across, 5)
        next_far(j, 0)

    def turn(t, carry):
        def stage(plan, work):
            turns, blocks = plan
            now = t == turns[0]
            for at_turn in turns[1:]:
                now = now | (t == at_turn)

            @pl.when(now)
            def _():
                index = 0
                for at_turn in turns:
                    index = index + jnp.where(t > at_turn, 1, 0)
                work((code(blocks) >> (3 * index)) % 8)

        stage(GATHER_DONE, gather_done)
        stage(SEND_NEAR, dispatch_near)
        stage(ONWARD, onward)
        stage(SPREAD, spread)
        stage(UNPACK, unpack)
        stage(COMPUTE, compute)
        stage(REDUCE, reduce_sides)
        stage(GO_HOME, go_home)
        stage(TURN_WEIGHTS, turn_weights)
        stage(WEIGHTS, weight_grads)
        return carry

    lax.fori_loop(0, TURNS, turn, 0)
    for q in range(len(WEIGHTS[0]), PARTS):
        weight_grads(q)

    for copy in dense_own() + dense_onward():
        copy.wait_send()

    def finish_far(j, carry):
        far_whole(j).wait_send()
        for copy in own_copies(j) + onward_copies(j):
            copy.wait_send()
        return carry

    lax.fori_loop(0, FAR, finish_far, 0)
    for n in range(NEAR):
        near_whole(n, 1 if near_block(n) == SAME else 0).wait_send()

    def finish_sides(p, carry):
        for s, side in ((0, right), (1, left)):
            pair_copy(s, p, side).wait_send()
            sum_copy(s, p, side).wait_send()
        return carry

    lax.fori_loop(0, ZS, finish_sides, 0)

    result = jnp.zeros((2 * tok_rows, half), jnp.float32)
    for p in GO_HOME[1]:
        z = (zi - offset(p) + ZS) % ZS
        some = home.at[pl.ds(0, plane - 1 if p == SAME else plane)]
        remote(some, some, home_out.at[p], home_sems.at[p], (right, rank)).wait_recv()
        block = home[at(z, plane)].reshape(plane * 2 * CAP, half)
        result += dot_rows(chosen(z, ones, ones), block)
    result = result.astype(jnp.bfloat16)
    out_tokens[:, pl.ds(0, half)] = result[:tok_rows]
    out_tokens[:, pl.ds(half, half)] = result[tok_rows:]

    def home_sent(p, count):
        some = pl.ds(0, count)
        remote(
            home_send.at[some], home.at[some], home_out.at[p], home_sems.at[p], (right, rank)
        ).wait_send()

    def finish(p, carry):
        @pl.when(p == SAME)
        def _():
            home_sent(p, plane - 1)

        @pl.when(p != SAME)
        def _():
            home_sent(p, plane)

        return carry

    lax.fori_loop(0, ZS, finish, 0)
    for q in range(PARTS):
        for copy in write_copies(q):
            copy.wait()


def write_out(*refs):
    count = (len(refs) - 1) // 2
    sources, targets, sems = refs[:count], refs[count : 2 * count], refs[-1]
    copies = []
    for number, (source, target) in enumerate(zip(sources, targets)):
        step = source.shape[0] // PARTS
        for piece in range(PARTS):
            lines = pl.ds(piece * step, step)
            copies.append(
                pltpu.make_async_copy(source.at[lines], target.at[lines], sems.at[number, piece])
            )
    for copy in copies:
        copy.start()
    for copy in copies:
        copy.wait()


def body(tokens, grad_out, route_weights, expert_ids, gate_weight, up_weight, down_weight):
    tok_rows, width = tokens.shape
    experts = lax.axis_size("expert")
    plane = XS * CORES
    rows = plane * CAP
    total = experts * CAP
    features, hidden = gate_weight.shape[1:]
    half = width // 2
    bf16, f32 = jnp.bfloat16, jnp.float32
    vmem, free = pl.BlockSpec(memory_space=pltpu.VMEM), pl.BlockSpec(memory_space=pl.ANY)
    hbm = pl.BlockSpec(memory_space=pltpu.HBM)
    dma = pltpu.SemaphoreType.DMA
    grads = pl.pallas_call(
        kernel,
        out_shape=(
            jax.ShapeDtypeStruct((tok_rows, width), bf16),
            jax.ShapeDtypeStruct((features, hidden), bf16),
            jax.ShapeDtypeStruct((features, hidden), bf16),
            jax.ShapeDtypeStruct((hidden, features), bf16),
        ),
        in_specs=[vmem, vmem, hbm, hbm, hbm],
        out_specs=(vmem, free, free, free),
        scratch_shapes=[
            pltpu.VMEM((PARTS, 2 * tok_rows, width), bf16),
            pltpu.VMEM((FAR, plane, 2 * CAP, width), bf16),
            pltpu.VMEM((FAR, plane, 2 * CAP, width), bf16),
            pltpu.VMEM((NEAR, plane, PARTS, 2 * CAP, width), bf16),
            pltpu.VMEM((NEAR, plane, PARTS, 2 * CAP, width), bf16),
            pltpu.VMEM((PARTS, total, width), bf16),
            pltpu.VMEM((PARTS, total, width), bf16),
            pltpu.VMEM((features, 2 * hidden), bf16),
            pltpu.VMEM((hidden, features), bf16),
            pltpu.VMEM((2 * hidden, features), bf16),
            pltpu.VMEM((features, hidden), bf16),
            pltpu.VMEM((total, 2 * hidden), bf16),
            pltpu.VMEM((total, hidden), bf16),
            pltpu.VMEM((hidden, total), bf16),
            pltpu.VMEM((SLOTS, 3, rows, width), f32),
            pltpu.VMEM((2, ZS, rows, half), bf16),
            pltpu.VMEM((2, ZS, rows, half), bf16),
            pltpu.VMEM((2, ZS, rows, width), bf16),
            pltpu.VMEM((2, ZS, rows, width), bf16),
            pltpu.VMEM((experts, 2 * CAP, half), bf16),
            pltpu.VMEM((experts, 2 * CAP, half), bf16),
            dma((3,)),
            dma((6,)),
            dma((6,)),
            dma((FAR,)),
            dma((FAR,)),
            dma((NEAR,)),
            dma((NEAR,)),
            dma((4, FAR)),
            dma((2, FAR)),
            dma((6, FAR)),
            dma((2, ZS)),
            dma((2, ZS)),
            dma((2, ZS)),
            dma((2, ZS)),
            dma((ZS,)),
            dma((ZS,)),
            dma((3, PARTS)),
        ],
        compiler_params=pltpu.CompilerParams(
            collective_id=0, has_side_effects=True, vmem_limit_bytes=47 * 1024 * 1024
        ),
    )(
        (2.0 * expert_ids.astype(f32) + route_weights.astype(f32)).T,
        jnp.concatenate([tokens, grad_out], axis=0),
        gate_weight[0], up_weight[0], down_weight[0],
    )
    grads = pl.pallas_call(
        write_out,
        out_shape=tuple(jax.ShapeDtypeStruct(array.shape, bf16) for array in grads),
        in_specs=[free] * 4,
        out_specs=(free,) * 4,
        scratch_shapes=[dma((4, PARTS))],
        compiler_params=pltpu.CompilerParams(vmem_limit_bytes=2 * 1024 * 1024),
    )(*grads)
    return (grads[0], grads[1][None], grads[2][None], grads[3][None])


def solution(mesh):
    placed = (
        P("expert", "dp"),
        P("expert", "dp"),
        P("expert", None),
        P("expert", None),
        P("expert", None, "dp"),
        P("expert", None, "dp"),
        P("expert", "dp", None),
    )
    return jax.shard_map(
        body,
        mesh=mesh,
        in_specs=placed,
        out_specs=(
            P("expert", "dp"),
            P("expert", None, "dp"),
            P("expert", None, "dp"),
            P("expert", "dp", None),
        ),
        check_vma=False,
    )
```

```python
import jax
import jax.numpy as jnp
from jax import lax
from jax.experimental import pallas as pl
from jax.experimental.pallas import tpu as pltpu
from jax.sharding import PartitionSpec as P

CAP = 8
PARTS = 4
ZS, XS, CORES = 8, 4, 2
MESH = pl.DeviceIdType.MESH

PLANE_OF = (5, 3, 2, 6, 0, 4, 7, 1)
FAR, NEAR, SAME = 5, 3, 4
SLOTS = 6


def code(items):
    return sum(item << (3 * place) for place, item in enumerate(items))


PLANE_CODE = code(PLANE_OF)

GATHER_DONE = ((2,), (4,))
SEND_NEAR = ((2, 3, 4, 5, 6, 7), (2, 4, 3, 5, 0, 1))
ONWARD = ((2, 3, 6, 7, 8), (3, 1, 0, 2, 4))
SPREAD = ((0, 1, 4, 5, 7), (3, 1, 0, 2, 4))
UNPACK = ((10, 15, 16), (0, 2, 1))
COMPUTE = ((7, 8, 10, 16), (0, 1, 2, 3))
REDUCE = ((8, 9, 10, 12, 13, 14, 18, 19), (1, 0, 2, 5, 4, 3, 6, 7))
GO_HOME = ((10, 11, 14, 16, 17, 20, 21, 22), (1, 0, 2, 5, 3, 6, 4, 7))
TURN_WEIGHTS = ((0, 1, 3, 5), (0, 1, 2, 3))
WEIGHTS = ((18, 19), (0, 1))
TURNS = 23


def dot_last(left, right):
    return lax.dot_general(
        left, right, (((1,), (1,)), ((), ())), preferred_element_type=jnp.float32
    )


def turned(block):
    size = block.shape[1]
    diagonal = lax.broadcasted_iota(jnp.int32, (size, size), 0) == (
        lax.broadcasted_iota(jnp.int32, (size, size), 1)
    )
    unit = jnp.where(diagonal, 1.0, 0.0).astype(jnp.bfloat16)
    return dot_last(unit, block).astype(jnp.bfloat16)


def dot_rows(left, right):
    return lax.dot_general(
        left, right, (((0,), (0,)), ((), ())), preferred_element_type=jnp.float32
    )


def kernel(
    table_ref, both_ref, gate_hbm, up_hbm, down_hbm,
    out_tokens, out_gate, out_up, out_down,
    dense, far_send, far_recv, near_send, near_recv, tok, sca, wgu, wdn, wgu_turned, wdn_turned, hid, act, act_turned, part,
    pair_send, pair_recv, sum_send, sum_recv, home_send, home,
    weight_sems, dense_out, dense_sems, far_out, far_sems, near_out, near_sems,
    own_out, onward_out, row_sems, pair_out, pair_sems, sum_out, sum_sems,
    home_out, home_sems, write_sems,
):
    rank = lax.axis_index("expert")
    y = lax.axis_index("dp")
    plane = XS * CORES
    experts = ZS * plane
    rows = plane * CAP
    zi, xi, ci = rank // plane, (rank // CORES) % XS, rank % CORES
    right, left = (y + 1) % PARTS, (y + PARTS - 1) % PARTS
    across = (y + 2) % PARTS
    tok_rows, width = both_ref.shape[0] // 2, both_ref.shape[1]
    half = width // 2
    hidden = act.shape[1]

    def at(row, col):
        return pl.ds(pl.multiple_of(row * col, col), col)

    def offset(p):
        return (PLANE_CODE >> (3 * p)) % 8

    def far_block(j):
        return j + j // 4

    def near_block(n):
        return 4 + n + (n + 1) // 2

    def peer(p, i, sign):
        z = (zi + sign * offset(p) + ZS) % ZS
        x = (xi + sign * (i // CORES) + XS) % XS
        c = (ci + i) % CORES
        return z * plane + x * CORES + c

    def remote(src, dst, out, arrive, device):
        return pltpu.make_async_remote_copy(
            src_ref=src, dst_ref=dst, send_sem=out, recv_sem=arrive,
            device_id=device, device_id_type=MESH,
        )

    barrier = pltpu.get_barrier_semaphore()

    def greet(j, carry):
        pl.semaphore_signal(
            barrier, inc=1, device_id=(y, (rank + j) % experts), device_id_type=MESH
        )
        return carry

    for side in (left, right):
        pl.semaphore_signal(barrier, inc=1, device_id=(side, rank), device_id_type=MESH)
    lax.fori_loop(1, experts, greet, 0)

    weight_copies = [
        pltpu.make_async_copy(gate_hbm, wgu.at[:, pl.ds(0, hidden)], weight_sems.at[0]),
        pltpu.make_async_copy(up_hbm, wgu.at[:, pl.ds(hidden, hidden)], weight_sems.at[1]),
        pltpu.make_async_copy(down_hbm, wdn, weight_sems.at[2]),
    ]
    for copy in weight_copies:
        copy.start()

    def dense_copy(h, q, out, arrive, side):
        some = pl.ds(h * tok_rows, tok_rows)
        return remote(
            both_ref.at[some] if q is y else dense.at[q, some], dense.at[q, some],
            out, dense_sems.at[arrive], (side, rank),
        )

    def dense_own():
        return [
            dense_copy(0, y, dense_out.at[0], 0, right),
            dense_copy(1, y, dense_out.at[1], 3, left),
            dense_copy(1, y, dense_out.at[2], 1, right),
            dense_copy(0, y, dense_out.at[3], 2, left),
        ]

    def dense_onward():
        return [
            dense_copy(0, left, dense_out.at[4], 4, right),
            dense_copy(1, right, dense_out.at[5], 5, left),
        ]

    def dense_arrival(h, q, arrive):
        dense_copy(h, q, dense_out.at[0], arrive, right).wait_recv()

    pl.semaphore_wait(barrier, experts + 1)
    for copy in dense_own():
        copy.start()
    dense[y] = both_ref[...]

    ids = jnp.floor(table_ref[...] * 0.5)
    weights = table_ref[...] - 2.0 * ids
    numbers = lax.broadcasted_iota(jnp.int32, (experts, tok_rows), 0).astype(jnp.float32)
    hits = [numbers == ids[c : c + 1] for c in range(2)]
    before = lax.broadcasted_iota(jnp.int32, (tok_rows, tok_rows), 0) < (
        lax.broadcasted_iota(jnp.int32, (tok_rows, tok_rows), 1)
    )
    earlier = jnp.dot(
        jnp.where(hits[0] | hits[1], 1.0, 0.0).astype(jnp.bfloat16),
        jnp.where(before, 1.0, 0.0).astype(jnp.bfloat16),
        preferred_element_type=jnp.float32,
    )
    place = [
        jnp.sum(jnp.where(hits[c], earlier, 0.0), axis=0, keepdims=True)
        + ids[c : c + 1] * (2 * CAP)
        for c in range(2)
    ]

    def chosen(z, first, second):
        line = lax.broadcasted_iota(jnp.int32, (plane * 2 * CAP, tok_rows), 0)
        line = (line + z * (plane * 2 * CAP)).astype(jnp.float32)
        halves = [
            jnp.where(line == place[0] + shift, value[0:1], 0.0)
            + jnp.where(line == place[1] + shift, value[1:2], 0.0)
            for shift, value in ((0.0, first), (float(CAP), second))
        ]
        return jnp.concatenate(halves, axis=1).astype(jnp.bfloat16)

    ones = jnp.ones_like(weights)

    def picks(p):
        return chosen((zi - offset(p) + ZS) % ZS, ones, weights)

    def pick(which, q):
        picked = jnp.dot(which, dense[q], preferred_element_type=jnp.float32)
        return picked.astype(jnp.bfloat16).reshape(plane, 2 * CAP, width)

    def far_copy(j, i):
        target = peer(far_block(j), i, -1)
        return remote(
            far_send.at[j, target % plane], far_recv.at[j, i],
            far_out.at[j], far_sems.at[j], (y, target),
        )

    def far_whole(j):
        return remote(far_send.at[j], far_recv.at[j], far_out.at[j], far_sems.at[j], (right, rank))

    def pack_far(j):
        far_send[j] = pick(picks(far_block(j)), y)

    def dispatch_far(j, carry):
        def one(i, inner):
            far_copy(j, i).start()
            return inner

        return lax.fori_loop(0, plane, one, carry)

    def near_copy(n, i):
        target = peer(near_block(n), i, -1)
        return remote(
            near_send.at[n, target % plane], near_recv.at[n, i],
            near_out.at[n], near_sems.at[n], (y, target),
        )

    def near_whole(n, first):
        some = pl.ds(first, plane - first)
        return remote(
            near_send.at[n, some], near_recv.at[n, some],
            near_out.at[n], near_sems.at[n], (right, rank),
        )

    def dispatch_near(m):
        n, second = m // 2, m % 2

        @pl.when(second == 0)
        def _():
            which = picks(near_block(n))
            for q in range(PARTS):
                near_send[n, :, q] = pick(which, q)

        def one(i, inner):
            near_copy(n, i).start()
            return inner

        @pl.when(m == 0)
        def _():
            near_recv[0, 0] = near_send[0, rank % plane]

        first = second * (plane // 2)
        lax.fori_loop(jnp.where(m == 0, 1, first), first + plane // 2, one, 0)

    def side_copy(buf, q, p, out, arrive, side):
        block = buf.at[q, at(p, rows)]
        return remote(block, block, out, arrive, (side, rank))

    def own_copies(j):
        p = far_block(j)
        return [
            side_copy(tok, y, p, own_out.at[0, j], row_sems.at[0, j], right),
            side_copy(sca, y, p, own_out.at[1, j], row_sems.at[3, j], left),
            side_copy(sca, y, p, own_out.at[2, j], row_sems.at[1, j], right),
            side_copy(tok, y, p, own_out.at[3, j], row_sems.at[2, j], left),
        ]

    def onward_copies(j):
        p = far_block(j)
        return [
            side_copy(tok, left, p, onward_out.at[0, j], row_sems.at[4, j], right),
            side_copy(sca, right, p, onward_out.at[1, j], row_sems.at[5, j], left),
        ]

    def arrival(buf, q, j, arrive):
        side_copy(
            buf, q, far_block(j), own_out.at[0, j], row_sems.at[arrive, j], right
        ).wait_recv()

    def separate(got, q, p):
        got = got.astype(jnp.float32)
        mine = at(p, rows)
        tok[q, mine, :] = got[:, :CAP, :].reshape(rows, width).astype(jnp.bfloat16)
        sca[q, mine, :] = got[:, CAP:, :].reshape(rows, width).astype(jnp.bfloat16)

    def spread(j):
        far_whole(j).wait_recv()
        separate(far_recv[j], y, far_block(j))
        for copy in own_copies(j):
            copy.start()

    def onward(j):
        copies = onward_copies(j)
        arrival(tok, left, j, 0)
        copies[0].start()
        arrival(sca, right, j, 3)
        copies[1].start()

    def unpack(n):
        p = near_block(n)

        @pl.when(p == SAME)
        def _():
            near_whole(n, 1).wait_recv()

        @pl.when(p != SAME)
        def _():
            near_whole(n, 0).wait_recv()

        for q in range(PARTS):
            separate(near_recv[n, :, q], q, p)

    def pair_copy(s, p, side):
        return remote(
            pair_send.at[s, p], pair_recv.at[s, p], pair_out.at[s, p], pair_sems.at[s, p],
            (side, rank),
        )

    def sum_copy(s, p, side):
        return remote(
            sum_send.at[s, p], sum_recv.at[s, p], sum_out.at[s, p], sum_sems.at[s, p],
            (side, rank),
        )

    def turn_weights(q):
        tile = min(256, width)

        def one(j, carry):
            lines = pl.ds(pl.multiple_of(q * width + j * tile, tile), tile)
            for h in range(2):
                some = pl.ds(h * hidden, hidden)
                wgu_turned[some, lines] = turned(wgu[lines, some])
            wdn_turned[lines, :] = turned(wdn[:, lines])
            return carry

        lax.fori_loop(0, width // tile, one, 0)

    def compute(pair):
        mine = at(pair, 2 * rows)

        def gathered(j):
            arrival(sca, left, j, 1)
            arrival(tok, right, j, 2)
            arrival(tok, across, j, 4)
            arrival(sca, across, j, 5)

        @pl.when(pair < 2)
        def _():
            gathered(2 * pair)
            gathered(2 * pair + 1)

        @pl.when(pair == 2)
        def _():
            gathered(4)

        pre = jnp.zeros((2 * rows, 2 * hidden), jnp.float32)
        grad_act = jnp.zeros((2 * rows, hidden), jnp.float32)
        for q in range(PARTS):
            pre += jnp.dot(
                tok[q, mine, :], wgu[pl.ds(q * width, width), :],
                preferred_element_type=jnp.float32,
            )
            grad_act += jnp.dot(
                sca[q, mine, :], wdn_turned[pl.ds(q * width, width), :],
                preferred_element_type=jnp.float32,
            )
        gate_pre, up_pre = pre[:, :hidden], pre[:, hidden:]
        sigmoid_gate = 1.0 / (1.0 + jnp.exp(-gate_pre))
        swish_gate = gate_pre * sigmoid_gate
        act[mine, :] = (swish_gate * up_pre).astype(jnp.bfloat16)
        hid[mine, :] = jnp.concatenate(
            [
                grad_act * up_pre * sigmoid_gate * (1.0 + gate_pre * (1.0 - sigmoid_gate)),
                grad_act * swish_gate,
            ],
            axis=1,
        ).astype(jnp.bfloat16)

        def back(q):
            return jnp.dot(
                hid[mine, :], wgu_turned[:, at(q, width)], preferred_element_type=jnp.float32
            )

        far = back(across).astype(jnp.bfloat16)
        for i in range(2):
            p = 2 * pair + i
            pair_send[0, p] = far[i * rows : (i + 1) * rows, :half]
            pair_send[1, p] = far[i * rows : (i + 1) * rows, half:]
            pair_copy(0, p, right).start()
            pair_copy(1, p, left).start()
        for kept, q in enumerate((right, left, y)):
            mine_part = back(q)
            for i in range(2):
                part[(2 * pair + i) % SLOTS, kept] = mine_part[i * rows : (i + 1) * rows]

    def reduce_sides(p):
        slot = p % SLOTS
        pair_copy(0, p, right).wait_recv()
        near = part[slot, 0]
        sum_send[0, p] = jnp.concatenate(
            [near[:, :half] + pair_recv[0, p].astype(jnp.float32), near[:, half:]], axis=1
        ).astype(jnp.bfloat16)
        sum_copy(0, p, right).start()
        pair_copy(1, p, left).wait_recv()
        near = part[slot, 1]
        sum_send[1, p] = jnp.concatenate(
            [near[:, :half], near[:, half:] + pair_recv[1, p].astype(jnp.float32)], axis=1
        ).astype(jnp.bfloat16)
        sum_copy(1, p, left).start()

    def home_copy(p, i):
        return remote(
            home_send.at[p * plane + i], home.at[rank], home_out.at[p], home_sems.at[p],
            (y, peer(p, i, 1)),
        )

    def go_home(p):
        sum_copy(0, p, right).wait_recv()
        sum_copy(1, p, left).wait_recv()
        total = (
            part[p % SLOTS, 2]
            + sum_recv[0, p].astype(jnp.float32)
            + sum_recv[1, p].astype(jnp.float32)
        ).reshape(plane, CAP, width)
        home_send[at(p, plane)] = jnp.concatenate(
            [total[:, :, :half], total[:, :, half:]], axis=1
        ).astype(jnp.bfloat16)

        def one(i, carry):
            home_copy(p, i).start()
            return carry

        @pl.when(p == SAME)
        def _():
            home[rank] = home_send[SAME * plane]
            lax.fori_loop(1, plane, one, 0)

        @pl.when(p != SAME)
        def _():
            lax.fori_loop(0, plane, one, 0)

    def write_copies(q):
        lines = at(q, width)
        return [
            pltpu.make_async_copy(
                wgu.at[lines, pl.ds(0, hidden)], out_gate.at[lines], write_sems.at[0, q]
            ),
            pltpu.make_async_copy(
                wgu.at[lines, pl.ds(hidden, hidden)], out_up.at[lines], write_sems.at[1, q]
            ),
            pltpu.make_async_copy(wdn.at[:, lines], out_down.at[:, lines], write_sems.at[2, q]),
        ]

    def weight_grads(q):
        tile = min(256, width)

        @pl.when(q == 0)
        def _():
            act_turned[...] = turned(act[...])

        def one(j, carry):
            cols = at(j, tile)
            lines = pl.ds(pl.multiple_of(q * width + j * tile, tile), tile)
            wgu[lines, :] = jnp.dot(
                turned(tok[q, :, cols]), hid[...], preferred_element_type=jnp.float32
            ).astype(jnp.bfloat16)
            wdn[:, lines] = jnp.dot(
                act_turned[...], sca[q, :, cols], preferred_element_type=jnp.float32
            ).astype(jnp.bfloat16)
            return carry

        lax.fori_loop(0, width // tile, one, 0)
        for copy in write_copies(q):
            copy.start()

    def next_far(j, carry):
        pack_far(j)
        return dispatch_far(j, carry)

    lax.fori_loop(1, 4, next_far, 0)
    copies = dense_onward()
    dense_arrival(0, left, 0)
    copies[0].start()
    dense_arrival(1, right, 3)
    copies[1].start()
    next_far(0, 0)
    for copy in weight_copies:
        copy.wait()

    def gather_done(j):
        dense_arrival(1, left, 1)
        dense_arrival(0, right, 2)
        dense_arrival(0, across, 4)
        dense_arrival(1, across, 5)
        next_far(j, 0)

    def turn(t, carry):
        def stage(plan, work):
            turns, blocks = plan
            now = t == turns[0]
            for at_turn in turns[1:]:
                now = now | (t == at_turn)

            @pl.when(now)
            def _():
                index = 0
                for at_turn in turns:
                    index = index + jnp.where(t > at_turn, 1, 0)
                work((code(blocks) >> (3 * index)) % 8)

        stage(GATHER_DONE, gather_done)
        stage(SEND_NEAR, dispatch_near)
        stage(ONWARD, onward)
        stage(SPREAD, spread)
        stage(UNPACK, unpack)
        stage(COMPUTE, compute)
        stage(REDUCE, reduce_sides)
        stage(GO_HOME, go_home)
        stage(TURN_WEIGHTS, turn_weights)
        stage(WEIGHTS, weight_grads)
        return carry

    lax.fori_loop(0, TURNS, turn, 0)
    for q in range(len(WEIGHTS[0]), PARTS):
        weight_grads(q)

    for copy in dense_own() + dense_onward():
        copy.wait_send()

    def finish_far(j, carry):
        far_whole(j).wait_send()
        for copy in own_copies(j) + onward_copies(j):
            copy.wait_send()
        return carry

    lax.fori_loop(0, FAR, finish_far, 0)
    for n in range(NEAR):
        near_whole(n, 1 if near_block(n) == SAME else 0).wait_send()

    def finish_sides(p, carry):
        for s, side in ((0, right), (1, left)):
            pair_copy(s, p, side).wait_send()
            sum_copy(s, p, side).wait_send()
        return carry

    lax.fori_loop(0, ZS, finish_sides, 0)

    result = jnp.zeros((2 * tok_rows, half), jnp.float32)
    for p in GO_HOME[1]:
        z = (zi - offset(p) + ZS) % ZS
        some = home.at[pl.ds(0, plane - 1 if p == SAME else plane)]
        remote(some, some, home_out.at[p], home_sems.at[p], (right, rank)).wait_recv()
        block = home[at(z, plane)].reshape(plane * 2 * CAP, half)
        result += dot_rows(chosen(z, ones, ones), block)
    result = result.astype(jnp.bfloat16)
    out_tokens[:, pl.ds(0, half)] = result[:tok_rows]
    out_tokens[:, pl.ds(half, half)] = result[tok_rows:]

    def home_sent(p, count):
        some = pl.ds(0, count)
        remote(
            home_send.at[some], home.at[some], home_out.at[p], home_sems.at[p], (right, rank)
        ).wait_send()

    def finish(p, carry):
        @pl.when(p == SAME)
        def _():
            home_sent(p, plane - 1)

        @pl.when(p != SAME)
        def _():
            home_sent(p, plane)

        return carry

    lax.fori_loop(0, ZS, finish, 0)
    for q in range(PARTS):
        for copy in write_copies(q):
            copy.wait()


def write_out(*refs):
    count = (len(refs) - 1) // 2
    sources, targets, sems = refs[:count], refs[count : 2 * count], refs[-1]
    copies = []
    for number, (source, target) in enumerate(zip(sources, targets)):
        step = source.shape[0] // PARTS
        for piece in range(PARTS):
            lines = pl.ds(piece * step, step)
            copies.append(
                pltpu.make_async_copy(source.at[lines], target.at[lines], sems.at[number, piece])
            )
    for copy in copies:
        copy.start()
    for copy in copies:
        copy.wait()


def body(tokens, grad_out, route_weights, expert_ids, gate_weight, up_weight, down_weight):
    tok_rows, width = tokens.shape
    experts = lax.axis_size("expert")
    plane = XS * CORES
    rows = plane * CAP
    total = experts * CAP
    features, hidden = gate_weight.shape[1:]
    half = width // 2
    bf16, f32 = jnp.bfloat16, jnp.float32
    vmem, free = pl.BlockSpec(memory_space=pltpu.VMEM), pl.BlockSpec(memory_space=pl.ANY)
    hbm = pl.BlockSpec(memory_space=pltpu.HBM)
    dma = pltpu.SemaphoreType.DMA
    grads = pl.pallas_call(
        kernel,
        out_shape=(
            jax.ShapeDtypeStruct((tok_rows, width), bf16),
            jax.ShapeDtypeStruct((features, hidden), bf16),
            jax.ShapeDtypeStruct((features, hidden), bf16),
            jax.ShapeDtypeStruct((hidden, features), bf16),
        ),
        in_specs=[vmem, vmem, hbm, hbm, hbm],
        out_specs=(vmem, free, free, free),
        scratch_shapes=[
            pltpu.VMEM((PARTS, 2 * tok_rows, width), bf16),
            pltpu.VMEM((FAR, plane, 2 * CAP, width), bf16),
            pltpu.VMEM((FAR, plane, 2 * CAP, width), bf16),
            pltpu.VMEM((NEAR, plane, PARTS, 2 * CAP, width), bf16),
            pltpu.VMEM((NEAR, plane, PARTS, 2 * CAP, width), bf16),
            pltpu.VMEM((PARTS, total, width), bf16),
            pltpu.VMEM((PARTS, total, width), bf16),
            pltpu.VMEM((features, 2 * hidden), bf16),
            pltpu.VMEM((hidden, features), bf16),
            pltpu.VMEM((2 * hidden, features), bf16),
            pltpu.VMEM((features, hidden), bf16),
            pltpu.VMEM((total, 2 * hidden), bf16),
            pltpu.VMEM((total, hidden), bf16),
            pltpu.VMEM((hidden, total), bf16),
            pltpu.VMEM((SLOTS, 3, rows, width), f32),
            pltpu.VMEM((2, ZS, rows, half), bf16),
            pltpu.VMEM((2, ZS, rows, half), bf16),
            pltpu.VMEM((2, ZS, rows, width), bf16),
            pltpu.VMEM((2, ZS, rows, width), bf16),
            pltpu.VMEM((experts, 2 * CAP, half), bf16),
            pltpu.VMEM((experts, 2 * CAP, half), bf16),
            dma((3,)),
            dma((6,)),
            dma((6,)),
            dma((FAR,)),
            dma((FAR,)),
            dma((NEAR,)),
            dma((NEAR,)),
            dma((4, FAR)),
            dma((2, FAR)),
            dma((6, FAR)),
            dma((2, ZS)),
            dma((2, ZS)),
            dma((2, ZS)),
            dma((2, ZS)),
            dma((ZS,)),
            dma((ZS,)),
            dma((3, PARTS)),
        ],
        compiler_params=pltpu.CompilerParams(
            collective_id=0, has_side_effects=True, vmem_limit_bytes=47 * 1024 * 1024
        ),
    )(
        (2.0 * expert_ids.astype(f32) + route_weights.astype(f32)).T,
        jnp.concatenate([tokens, grad_out], axis=0),
        gate_weight[0], up_weight[0], down_weight[0],
    )
    grads = pl.pallas_call(
        write_out,
        out_shape=tuple(jax.ShapeDtypeStruct(array.shape, bf16) for array in grads),
        in_specs=[free] * 4,
        out_specs=(free,) * 4,
        scratch_shapes=[dma((4, PARTS))],
        compiler_params=pltpu.CompilerParams(vmem_limit_bytes=2 * 1024 * 1024),
    )(*grads)
    return (grads[0], grads[1][None], grads[2][None], grads[3][None])


def solution(mesh):
    placed = (
        P("expert", "dp"),
        P("expert", "dp"),
        P("expert", None),
        P("expert", None),
        P("expert", None, "dp"),
        P("expert", None, "dp"),
        P("expert", "dp", None),
    )
    return jax.shard_map(
        body,
        mesh=mesh,
        in_specs=placed,
        out_specs=(
            P("expert", "dp"),
            P("expert", None, "dp"),
            P("expert", None, "dp"),
            P("expert", "dp", None),
        ),
        check_vma=False,
    )
```
